32 devices in a mesh: mem: 4 (over z), lat: 2 (over x), lon: 4 (over y, core).
Axes of the slice: x: 2, y: 2, z: 4, core: 2. Of those that a mesh axis runs over, the one named last changes fastest.
Arguments:
- gradient: float32 [4, 64, 1024], P('mem', 'lat', 'lon'), may hold values from -6 to 6
- perturbations: bfloat16 [20, 4, 64, 1024], P('mem', None, 'lat', 'lon'), may hold values from -6 to 6
- filter_coef: float32 [5, 64, 1024], P(None, 'lat', 'lon'), may hold values from 0.1 to 0.6
Outputs:
- hess_grad: float32 [4, 64, 1024], P('mem', 'lat', 'lon')
The draws below stay inside these ranges and needn't reach their ends.
All inputs are finite; a program needn't handle non-finite values.
Results may differ from the reference program's by a relative error of at most 0.0003.
Values may be sent and summed in bfloat16 or wider, within the bound.
A program may use at most 64 MiB of HBM per device.

```python
import jax
import jax.numpy as jnp
from jax import lax

MEMBERS = 20
LEV = 4
NLAT = 64
NLON = 1024


def block_scale(own_key, dims, split, least, top_value):
    gain, own = 1.0, jax.random.fold_in(own_key, 6)
    for dim, blocks in split:
        steps = jnp.exp(jax.random.uniform(jax.random.fold_in(own, dim), (blocks,), jnp.float32, least / len(split), top_value / len(split)))
        gain = gain * jnp.repeat(steps, dims[dim] // blocks).reshape([-1 if axis == dim else 1 for axis in range(len(dims))])
    return gain


def centred(key, extent, deviation, most, split=(), kind=jnp.bfloat16):
    loudness = block_scale(key, extent, split, -0.22, 0.18) if split else 1.0
    result = jax.random.normal(key, extent, jnp.float32) * deviation * loudness
    return jnp.minimum(jnp.maximum(result, -most), most).astype(kind)


def setup_inputs(seed: int = 0) -> dict:
    key_of = jax.random.split(jax.random.key(seed), 4)
    gradient = centred(key_of[0], (LEV, NLAT, NLON), 1.0, 6.0, ((0, 4), (1, 2), (2, 4)), jnp.float32)
    perturbations = centred(key_of[1], (MEMBERS, LEV, NLAT, NLON), 1.0, 6.0, ((0, 4), (2, 2), (3, 4)))
    filter_coef = jnp.clip(0.1 + 0.5 * jax.random.uniform(key_of[2], (5, NLAT, NLON), jnp.float32) ** block_scale(key_of[2], (5, NLAT, NLON), ((1, 2), (2, 4)), -0.2, 0.2), 0.1, 0.6)
    return dict(gradient=gradient, perturbations=perturbations, filter_coef=filter_coef)


def forward_pass(values, filter_coef):
    padded = jnp.pad(values, ((0, 0), (1, 1), (1, 1)))
    out = filter_coef[0] * values + filter_coef[1] * padded[:, :-2, 1:-1]
    out = out + filter_coef[2] * padded[:, 2:, 1:-1]
    out = out + filter_coef[3] * padded[:, 1:-1, :-2]
    return out + filter_coef[4] * padded[:, 1:-1, 2:]


def adjoint_pass(values, filter_coef):
    widths = ((0, 0), (1, 1), (1, 1))
    north_term = jnp.pad(filter_coef[1] * values, widths)
    south_term = jnp.pad(filter_coef[2] * values, widths)
    west_term = jnp.pad(filter_coef[3] * values, widths)
    east_term = jnp.pad(filter_coef[4] * values, widths)
    out = filter_coef[0] * values + north_term[:, 2:, 1:-1] + south_term[:, :-2, 1:-1]
    return out + west_term[:, 1:-1, 2:] + east_term[:, 1:-1, :-2]


def reference(gradient, perturbations, filter_coef):
    def member_step(summed, member_pert):
        member_vals = member_pert.astype(jnp.float32)
        product = member_vals * gradient
        product = adjoint_pass(adjoint_pass(product, filter_coef), filter_coef)
        product = forward_pass(forward_pass(product, filter_coef), filter_coef)
        return summed + member_vals * product, None

    summed, unused = lax.scan(member_step, jnp.zeros(gradient.shape, jnp.float32), perturbations)
    return summed * (1.0 / (MEMBERS - 1))
```

```python
import functools

import jax
import jax.numpy as jnp
from jax import lax
from jax.experimental import pallas as pl
from jax.experimental.pallas import tpu as pltpu
from jax.sharding import PartitionSpec as P

HALO = 4
LANES = 128
SUB = 8
QUAD = 4
DIRECTIONS = ((-1, 0), (1, 0), (0, -1), (0, 1), (-1, -1), (-1, 1), (1, -1), (1, 1))


def shifted(values, offset, axis):
    return pltpu.roll(values, (-offset) % values.shape[axis], axis)


def circular(centre_rows, north_rows, south_rows, row_low):
    return jnp.concatenate([centre_rows, jnp.where(row_low, south_rows, north_rows)], axis=0)


def folded(padded, cols):
    low = lax.broadcasted_iota(jnp.int32, (padded.shape[0], LANES), 1) < LANES // 2
    side = jnp.where(low, padded[:, LANES + cols :], padded[:, :LANES])
    return jnp.concatenate([padded[:, LANES : LANES + cols], side], axis=1)


def kernel(
    sizes,
    pert,
    grad,
    coef,
    out,
    centre,
    field,
    send_rows,
    send_cols,
    recv_rows,
    recv_cols,
    ext,
    stencils,
    scaled,
    z_send,
    z_recv,
    halo_send,
    halo_recv,
    local_sem,
):
    mem_count, lat_count, lon_count, scale = sizes
    per_mem, _, rows, cols = pert.shape
    members = centre.shape[0]
    mem, lat, lon = (lax.axis_index(name) for name in ("mem", "lat", "lon"))
    mesh_id = pl.DeviceIdType.MESH

    def present(direction):
        up, right = direction
        checks = []
        if up:
            checks.append(lat > 0 if up < 0 else lat < lat_count - 1)
        if right:
            checks.append(lon > 0 if right < 0 else lon < lon_count - 1)
        return functools.reduce(jnp.logical_and, checks)

    def neighbour(direction):
        return (mem, lat + direction[0], lon + direction[1])

    def peer(offset):
        return lax.rem(mem + offset, mem_count)

    barrier = pltpu.get_barrier_semaphore()
    for offset in range(1, mem_count):
        pl.semaphore_signal(barrier, inc=1, device_id=(peer(offset), lat, lon), device_id_type=mesh_id)
    for direction in DIRECTIONS:

        @pl.when(present(direction))
        def _():
            pl.semaphore_signal(barrier, inc=1, device_id=neighbour(direction), device_id_type=mesh_id)

    own_pert = pltpu.make_async_copy(
        pert.at[:, mem], centre.at[pl.ds(mem * per_mem, per_mem)], local_sem.at[0]
    )
    own_pert.start()
    inner_rows, inner_cols = pl.ds(SUB, rows), pl.ds(LANES, cols)
    own_coef = pltpu.make_async_copy(
        coef, ext.at[pl.ds(0, 5), inner_rows, inner_cols], local_sem.at[1]
    )
    own_coef.start()
    own_grad = pltpu.make_async_copy(
        grad, ext.at[pl.ds(5, 1), inner_rows, inner_cols], local_sem.at[2]
    )
    own_grad.start()

    blocks = [
        1 + jnp.where(here > 0, 1, 0) + jnp.where(here < count - 1, 1, 0)
        for here, count in ((lat, lat_count), (lon, lon_count))
    ]
    pl.semaphore_wait(barrier, mem_count - 2 + blocks[0] * blocks[1])

    def across(offset):
        target = peer(offset)
        return pltpu.make_async_remote_copy(
            src_ref=pert.at[:, target],
            dst_ref=centre.at[pl.ds(mem * per_mem, per_mem)],
            send_sem=z_send.at[offset - 1],
            recv_sem=z_recv.at[offset - 1],
            device_id=(target, lat, lon),
            device_id_type=mesh_id,
        )

    def arriving(offset):
        source = peer(mem_count - offset)
        return pltpu.make_async_remote_copy(
            src_ref=pert.at[:, source],
            dst_ref=centre.at[pl.ds(source * per_mem, per_mem)],
            send_sem=z_send.at[offset - 1],
            recv_sem=z_recv.at[offset - 1],
            device_id=(source, lat, lon),
            device_id_type=mesh_id,
        )

    for offset in range(1, mem_count):
        across(offset).start()

    def span(step, low, size, edge):
        if step == 0:
            return pl.ds(0, size), pl.ds(low, size)
        if step < 0:
            return pl.ds(0, edge), pl.ds(low + size, edge)
        return pl.ds(size - edge, edge), pl.ds(low - edge, edge)

    def fixed_copies(number, direction):
        source_rows, target_rows = span(direction[0], SUB, rows, SUB)
        source_cols, target_cols = span(direction[1], LANES, cols, LANES)
        common = dict(device_id=neighbour(direction), device_id_type=mesh_id)
        return [
            pltpu.make_async_remote_copy(
                src_ref=coef.at[:, source_rows, source_cols],
                dst_ref=ext.at[pl.ds(0, 5), target_rows, target_cols],
                send_sem=halo_send.at[0, number],
                recv_sem=halo_recv.at[0, number],
                **common,
            ),
            pltpu.make_async_remote_copy(
                src_ref=grad.at[:, source_rows, source_cols],
                dst_ref=ext.at[pl.ds(5, 1), target_rows, target_cols],
                send_sem=halo_send.at[1, number],
                recv_sem=halo_recv.at[1, number],
                **common,
            ),
        ]

    def pert_copy(number, direction):
        up, right = direction
        if up == 0:
            side = 0 if right < 0 else 1
            source, target = send_cols.at[side], recv_cols.at[side]
        else:
            side = 0 if up < 0 else 1
            source_cols, target_cols = span(right, LANES, cols, LANES)
            source = send_rows.at[side, :, source_cols]
            target = recv_rows.at[side, :, target_cols]
        return pltpu.make_async_remote_copy(
            src_ref=source,
            dst_ref=target,
            send_sem=halo_send.at[2, number],
            recv_sem=halo_recv.at[2, number],
            device_id=neighbour(direction),
            device_id_type=mesh_id,
        )

    for number, direction in enumerate(DIRECTIONS):

        @pl.when(present(direction))
        def _():
            for copy in fixed_copies(number, direction):
                copy.start()

    own_pert.wait()
    for offset in range(1, mem_count):
        arriving(offset).wait_recv()

    low_row = lax.broadcasted_iota(jnp.int32, (SUB, cols), 0) < HALO
    lane = lax.broadcasted_iota(jnp.int32, (rows, LANES), 1)

    def pack(quad, carry):
        tops, bottoms = [], []
        west = east = None
        for k in range(QUAD):
            block = centre[quad * QUAD + k].astype(jnp.float32)
            tops.append(block[:SUB])
            bottoms.append(block[rows - SUB :])
            place = (lane >= HALO * k) & (lane < HALO * (k + 1))
            first = pltpu.roll(block[:, :LANES], HALO * k, 1) if k else block[:, :LANES]
            last = pltpu.roll(block[:, cols - LANES :], HALO * (k + 1), 1)
            west = first if west is None else jnp.where(place, first, west)
            east = last if east is None else jnp.where(place, last, east)
        top_tiles = [
            jnp.where(low_row, tops[k], pltpu.roll(tops[k + 1], HALO, 0)) for k in (0, 2)
        ]
        bottom_tiles = [
            jnp.where(low_row, pltpu.roll(bottoms[k + 1], HALO, 0), bottoms[k]) for k in (0, 2)
        ]
        here = pl.ds(pl.multiple_of(quad * 2 * SUB, 2 * SUB), 2 * SUB)
        send_rows[0, here, :] = jnp.concatenate(top_tiles, axis=0).astype(jnp.bfloat16)
        send_rows[1, here, :] = jnp.concatenate(bottom_tiles, axis=0).astype(jnp.bfloat16)
        send_cols[0, quad] = west.astype(jnp.bfloat16)
        send_cols[1, quad] = east.astype(jnp.bfloat16)
        return carry

    lax.fori_loop(0, members // QUAD, pack, 0)

    for number, direction in enumerate(DIRECTIONS):

        @pl.when(present(direction))
        def _():
            pert_copy(number, direction).start()

    own_coef.wait()
    own_grad.wait()
    for number, direction in enumerate(DIRECTIONS):
        source = (-direction[0], -direction[1])

        @pl.when(present(source))
        def _():
            for copy in fixed_copies(number, direction):
                copy.wait_recv()

    full_rows, full_cols = rows + 2 * HALO, cols + LANES
    row_index = lax.broadcasted_iota(jnp.int32, (full_rows, full_cols), 0)
    col_index = lax.broadcasted_iota(jnp.int32, (full_rows, full_cols), 1)
    row_index = jnp.where(row_index < rows + HALO, row_index, row_index - full_rows)
    col_index = jnp.where(col_index < cols + LANES // 2, col_index, col_index - full_cols)
    near = (col_index >= -HALO) & (col_index < cols + HALO)
    row_index = row_index + lat * rows
    col_index = col_index + lon * cols
    inside = (
        near
        & (row_index >= 0)
        & (row_index < rows * lat_count)
        & (col_index >= 0)
        & (col_index < cols * lon_count)
    )
    low_row_full = lax.broadcasted_iota(jnp.int32, (SUB, full_cols), 0) < HALO

    def extended(index):
        wide = folded(ext[index], cols)
        wide = circular(
            wide[SUB : SUB + rows], wide[:SUB], wide[SUB + rows :], low_row_full
        )
        return jnp.where(inside, wide, 0.0)

    c0, cn, cs, cw, ce = (extended(index) for index in range(5))
    for index, value in enumerate((c0, cn, cs, cw, ce)):
        stencils[index] = value
    for index, value in enumerate(
        (shifted(cs, -1, 0), shifted(cn, 1, 0), shifted(ce, -1, 1), shifted(cw, 1, 1))
    ):
        stencils[5 + index] = jnp.where(inside, value, 0.0)
    scaled[0] = extended(5)
    scaled[1] = inside.astype(jnp.float32)

    for number, direction in enumerate(DIRECTIONS):
        source = (-direction[0], -direction[1])

        @pl.when(present(source))
        def _():
            pert_copy(number, direction).wait_recv()

    out[0] = jnp.zeros((rows, cols), jnp.float32)

    def one_pass(values, first):
        total = stencils[0] * values + stencils[first] * shifted(values, -1, 0)
        total = total + stencils[first + 1] * shifted(values, 1, 0)
        total = total + stencils[first + 2] * shifted(values, -1, 1)
        return total + stencils[first + 3] * shifted(values, 1, 1)

    def work(quad, carry):
        here = pl.ds(pl.multiple_of(quad * 2 * SUB, 2 * SUB), 2 * SUB)
        south = folded(recv_rows[0, here, :].astype(jnp.float32), cols)
        north = folded(recv_rows[1, here, :].astype(jnp.float32), cols)
        from_east = recv_cols[0, quad].astype(jnp.float32)
        from_west = recv_cols[1, quad].astype(jnp.float32)
        for k in range(QUAD):
            block = centre[quad * QUAD + k].astype(jnp.float32)
            tile = slice((k // 2) * SUB, (k // 2 + 1) * SUB)
            south_rows, north_rows = south[tile], north[tile]
            if k % 2:
                south_rows = pltpu.roll(south_rows, HALO, 0)
                north_rows = pltpu.roll(north_rows, HALO, 0)
            east = pltpu.roll(from_east, LANES - HALO * k, 1) if k else from_east
            west = pltpu.roll(from_west, LANES - HALO * (k + 1), 1)
            side = jnp.where(lane < LANES // 2, east, west)
            field[k] = circular(
                jnp.concatenate([block, side], axis=1), north_rows, south_rows, low_row_full
            )
        for k in range(QUAD):
            values = jnp.where(scaled[1] > 0.5, field[k] * scaled[0], 0.0)
            values = one_pass(values, 5)
            values = one_pass(values, 5)
            values = one_pass(values, 1)
            values = one_pass(values, 1)
            out[0] += values[:rows, :cols] * field[k, :rows, :cols]
        return carry

    lax.fori_loop(0, members // QUAD, work, 0)
    out[0] = out[0] * scale

    for offset in range(1, mem_count):
        across(offset).wait_send()
    for number, direction in enumerate(DIRECTIONS):

        @pl.when(present(direction))
        def _():
            for copy in fixed_copies(number, direction):
                copy.wait_send()
            pert_copy(number, direction).wait_send()


def body(mesh_sizes, gradient, perturbations, filter_coef):
    mem_count, lat_count, lon_count = mesh_sizes
    levels, rows, cols = gradient.shape
    members = perturbations.shape[0] * mem_count
    assert levels == 1 and members % QUAD == 0 and rows % 16 == 0 and cols % LANES == 0
    full_rows, full_cols = rows + 2 * HALO, cols + LANES
    packed = members // QUAD * 2 * SUB
    sizes = (mem_count, lat_count, lon_count, 1.0 / (members - 1))
    return pl.pallas_call(
        functools.partial(kernel, sizes),
        out_shape=jax.ShapeDtypeStruct(gradient.shape, jnp.float32),
        in_specs=[pl.BlockSpec(memory_space=pl.ANY)] * 3,
        out_specs=pl.BlockSpec(memory_space=pltpu.VMEM),
        scratch_shapes=[
            pltpu.VMEM((members, rows, cols), jnp.bfloat16),
            pltpu.VMEM((QUAD, full_rows, full_cols), jnp.float32),
            pltpu.VMEM((2, packed, cols), jnp.bfloat16),
            pltpu.VMEM((2, members // QUAD, rows, LANES), jnp.bfloat16),
            pltpu.VMEM((2, packed, cols + 2 * LANES), jnp.bfloat16),
            pltpu.VMEM((2, members // QUAD, rows, LANES), jnp.bfloat16),
            pltpu.VMEM((6, rows + 2 * SUB, cols + 2 * LANES), jnp.float32),
            pltpu.VMEM((9, full_rows, full_cols), jnp.float32),
            pltpu.VMEM((2, full_rows, full_cols), jnp.float32),
            pltpu.SemaphoreType.DMA((max(1, mem_count - 1),)),
            pltpu.SemaphoreType.DMA((max(1, mem_count - 1),)),
            pltpu.SemaphoreType.DMA((3, len(DIRECTIONS))),
            pltpu.SemaphoreType.DMA((3, len(DIRECTIONS))),
            pltpu.SemaphoreType.DMA((3,)),
        ],
        compiler_params=pltpu.CompilerParams(
            collective_id=0, has_side_effects=True, vmem_limit_bytes=32 * 1024 * 1024
        ),
    )(perturbations, gradient, filter_coef)


def solution(mesh):
    sizes = tuple(mesh.shape[name] for name in ("mem", "lat", "lon"))
    return jax.shard_map(
        functools.partial(body, sizes),
        mesh=mesh,
        in_specs=(P("mem", "lat", "lon"), P("mem", None, "lat", "lon"), P(None, "lat", "lon")),
        out_specs=P("mem", "lat", "lon"),
        check_vma=False,
    )
```

```python
import functools

import jax
import jax.numpy as jnp
from jax import lax
from jax.experimental import pallas as pl
from jax.experimental.pallas import tpu as pltpu
from jax.sharding import PartitionSpec as P

HALO = 4
LANES = 128
SUB = 8
DIRECTIONS = ((-1, 0), (1, 0), (0, -1), (0, 1), (-1, -1), (-1, 1), (1, -1), (1, 1))


def shifted(values, offset, axis):
    return pltpu.roll(values, (-offset) % values.shape[axis], axis)


def circular(centre_rows, north_rows, south_rows, row_low):
    return jnp.concatenate([centre_rows, jnp.where(row_low, south_rows, north_rows)], axis=0)


def folded(padded, cols):
    low = lax.broadcasted_iota(jnp.int32, (padded.shape[0], LANES), 1) < LANES // 2
    side = jnp.where(low, padded[:, LANES + cols :], padded[:, :LANES])
    return jnp.concatenate([padded[:, LANES : LANES + cols], side], axis=1)


def kernel(
    sizes,
    pert,
    grad,
    coef,
    out,
    centre,
    field,
    send_rows,
    send_cols,
    recv_rows,
    recv_cols,
    ext,
    stencils,
    scaled,
    z_send,
    z_recv,
    halo_send,
    halo_recv,
    local_sem,
):
    mem_count, lat_count, lon_count, scale = sizes
    per_mem, _, rows, cols = pert.shape
    mem, lat, lon = (lax.axis_index(name) for name in ("mem", "lat", "lon"))
    mesh_id = pl.DeviceIdType.MESH

    def present(direction):
        up, right = direction
        checks = []
        if up:
            checks.append(lat > 0 if up < 0 else lat < lat_count - 1)
        if right:
            checks.append(lon > 0 if right < 0 else lon < lon_count - 1)
        return functools.reduce(jnp.logical_and, checks)

    def neighbour(direction):
        return (mem, lat + direction[0], lon + direction[1])

    def peer(offset):
        total, bit = 0, 1
        while bit < mem_count:
            total = total + bit * lax.rem(lax.div(mem, bit) + lax.div(offset, bit), 2)
            bit *= 2
        return total

    def group_at(step):
        if mem_count < 3:
            return step
        return jnp.where(step == 0, 0, lax.rem(step, mem_count - 1) + 1)

    barrier = pltpu.get_barrier_semaphore()
    for offset in range(1, mem_count):
        pl.semaphore_signal(barrier, inc=1, device_id=(peer(jnp.int32(offset)), lat, lon), device_id_type=mesh_id)
    for direction in DIRECTIONS:

        @pl.when(present(direction))
        def _():
            pl.semaphore_signal(barrier, inc=1, device_id=neighbour(direction), device_id_type=mesh_id)

    own_pert = pltpu.make_async_copy(
        pert.at[:, mem], centre.at[0], local_sem.at[0]
    )
    own_pert.start()
    inner_rows, inner_cols = pl.ds(SUB, rows), pl.ds(LANES, cols)
    own_coef = pltpu.make_async_copy(
        coef, ext.at[pl.ds(0, 5), inner_rows, inner_cols], local_sem.at[1]
    )
    own_coef.start()
    own_grad = pltpu.make_async_copy(
        grad, ext.at[pl.ds(5, 1), inner_rows, inner_cols], local_sem.at[2]
    )
    own_grad.start()

    blocks = [
        1 + jnp.where(here > 0, 1, 0) + jnp.where(here < count - 1, 1, 0)
        for here, count in ((lat, lat_count), (lon, lon_count))
    ]
    pl.semaphore_wait(barrier, mem_count - 2 + blocks[0] * blocks[1])

    def across(offset):
        target = peer(offset)
        return pltpu.make_async_remote_copy(
            src_ref=pert.at[:, target],
            dst_ref=centre.at[offset],
            send_sem=z_send.at[offset],
            recv_sem=z_recv.at[offset],
            device_id=(target, lat, lon),
            device_id_type=mesh_id,
        )

    for step in range(1, mem_count):
        across(group_at(jnp.int32(step))).start()

    def span(step, low, size, edge):
        if step == 0:
            return pl.ds(0, size), pl.ds(low, size)
        if step < 0:
            return pl.ds(0, edge), pl.ds(low + size, edge)
        return pl.ds(size - edge, edge), pl.ds(low - edge, edge)

    def fixed_copies(number, direction):
        source_rows, target_rows = span(direction[0], SUB, rows, SUB)
        source_cols, target_cols = span(direction[1], LANES, cols, LANES)
        common = dict(device_id=neighbour(direction), device_id_type=mesh_id)
        return [
            pltpu.make_async_remote_copy(
                src_ref=coef.at[:, source_rows, source_cols],
                dst_ref=ext.at[pl.ds(0, 5), target_rows, target_cols],
                send_sem=halo_send.at[0, number],
                recv_sem=halo_recv.at[0, number],
                **common,
            ),
            pltpu.make_async_remote_copy(
                src_ref=grad.at[:, source_rows, source_cols],
                dst_ref=ext.at[pl.ds(5, 1), target_rows, target_cols],
                send_sem=halo_send.at[1, number],
                recv_sem=halo_recv.at[1, number],
                **common,
            ),
        ]

    def pert_copy(group, number, direction):
        up, right = direction
        if up == 0:
            side = 0 if right < 0 else 1
            source, target = send_cols.at[group, side], recv_cols.at[group, side]
        else:
            side = 0 if up < 0 else 1
            source_cols, target_cols = span(right, LANES, cols, LANES)
            source = send_rows.at[group, side, :, source_cols]
            target = recv_rows.at[group, side, :, target_cols]
        return pltpu.make_async_remote_copy(
            src_ref=source,
            dst_ref=target,
            send_sem=halo_send.at[2 + group, number],
            recv_sem=halo_recv.at[2 + group, number],
            device_id=neighbour(direction),
            device_id_type=mesh_id,
        )

    for number, direction in enumerate(DIRECTIONS):

        @pl.when(present(direction))
        def _():
            for copy in fixed_copies(number, direction):
                copy.start()

    low_row = lax.broadcasted_iota(jnp.int32, (SUB, cols), 0) < HALO
    lane = lax.broadcasted_iota(jnp.int32, (rows, LANES), 1)
    tiles = send_rows.shape[2] // SUB

    def pack(group):
        tops, bottoms = [], []
        west = east = None
        for k in range(per_mem):
            block = centre[group, k].astype(jnp.float32)
            top, bottom = block[:SUB], block[rows - SUB :]
            if k % 2:
                tops[-1] = jnp.where(low_row, tops[-1], pltpu.roll(top, HALO, 0))
                bottoms[-1] = jnp.where(low_row, pltpu.roll(bottom, HALO, 0), bottoms[-1])
            else:
                tops.append(top)
                bottoms.append(bottom)
            place = (lane >= HALO * k) & (lane < HALO * (k + 1))
            first = pltpu.roll(block[:, :LANES], HALO * k, 1) if k else block[:, :LANES]
            last = pltpu.roll(block[:, cols - LANES :], HALO * (k + 1) % LANES, 1)
            west = first if west is None else jnp.where(place, first, west)
            east = last if east is None else jnp.where(place, last, east)
        while len(tops) < tiles:
            tops.append(tops[-1])
            bottoms.append(bottoms[-1])
        send_rows[group, 0] = jnp.concatenate(tops, axis=0).astype(jnp.bfloat16)
        send_rows[group, 1] = jnp.concatenate(bottoms, axis=0).astype(jnp.bfloat16)
        send_cols[group, 0] = west.astype(jnp.bfloat16)
        send_cols[group, 1] = east.astype(jnp.bfloat16)
        for number, direction in enumerate(DIRECTIONS):

            @pl.when(present(direction))
            def _():
                pert_copy(group, number, direction).start()

    own_pert.wait()
    pack(jnp.int32(0))

    own_coef.wait()
    own_grad.wait()
    for number, direction in enumerate(DIRECTIONS):
        source = (-direction[0], -direction[1])

        @pl.when(present(source))
        def _():
            for copy in fixed_copies(number, direction):
                copy.wait_recv()

    full_rows, full_cols = rows + 2 * HALO, cols + LANES
    row_index = lax.broadcasted_iota(jnp.int32, (full_rows, full_cols), 0)
    col_index = lax.broadcasted_iota(jnp.int32, (full_rows, full_cols), 1)
    row_index = jnp.where(row_index < rows + HALO, row_index, row_index - full_rows)
    col_index = jnp.where(col_index < cols + LANES // 2, col_index, col_index - full_cols)
    near = (col_index >= -HALO) & (col_index < cols + HALO)
    row_index = row_index + lat * rows
    col_index = col_index + lon * cols
    inside = (
        near
        & (row_index >= 0)
        & (row_index < rows * lat_count)
        & (col_index >= 0)
        & (col_index < cols * lon_count)
    )
    low_row_full = lax.broadcasted_iota(jnp.int32, (SUB, full_cols), 0) < HALO

    def extended(index):
        wide = folded(ext[index], cols)
        wide = circular(
            wide[SUB : SUB + rows], wide[:SUB], wide[SUB + rows :], low_row_full
        )
        return jnp.where(inside, wide, 0.0)

    c0, cn, cs, cw, ce = (extended(index) for index in range(5))
    for index, value in enumerate((c0, cn, cs, cw, ce)):
        stencils[index] = value
    for index, value in enumerate(
        (shifted(cs, -1, 0), shifted(cn, 1, 0), shifted(ce, -1, 1), shifted(cw, 1, 1))
    ):
        stencils[5 + index] = jnp.where(inside, value, 0.0)
    scaled[0] = extended(5)
    scaled[1] = inside.astype(jnp.float32)

    out[0] = jnp.zeros((rows, cols), jnp.float32)

    def one_pass(values, first):
        total = stencils[0] * values + stencils[first] * shifted(values, -1, 0)
        total = total + stencils[first + 1] * shifted(values, 1, 0)
        total = total + stencils[first + 2] * shifted(values, -1, 1)
        return total + stencils[first + 3] * shifted(values, 1, 1)

    def work(group):
        for number, direction in enumerate(DIRECTIONS):
            source = (-direction[0], -direction[1])

            @pl.when(present(source))
            def _():
                pert_copy(group, number, direction).wait_recv()

        south = folded(recv_rows[group, 0].astype(jnp.float32), cols)
        north = folded(recv_rows[group, 1].astype(jnp.float32), cols)
        from_east = recv_cols[group, 0].astype(jnp.float32)
        from_west = recv_cols[group, 1].astype(jnp.float32)
        for k in range(per_mem):
            block = centre[group, k].astype(jnp.float32)
            tile = slice((k // 2) * SUB, (k // 2 + 1) * SUB)
            south_rows, north_rows = south[tile], north[tile]
            if k % 2:
                south_rows = pltpu.roll(south_rows, HALO, 0)
                north_rows = pltpu.roll(north_rows, HALO, 0)
            east = pltpu.roll(from_east, LANES - HALO * k, 1) if k else from_east
            west = pltpu.roll(from_west, (-HALO * (k + 1)) % LANES, 1)
            side = jnp.where(lane < LANES // 2, east, west)
            field[k] = circular(
                jnp.concatenate([block, side], axis=1), north_rows, south_rows, low_row_full
            )
        for k in range(per_mem):
            values = jnp.where(scaled[1] > 0.5, field[k] * scaled[0], 0.0)
            values = one_pass(values, 5)
            values = one_pass(values, 5)
            values = one_pass(values, 1)
            values = one_pass(values, 1)
            out[0] += values[:rows, :cols] * field[k, :rows, :cols]

    def step_work(step, carry):
        @pl.when(step + 1 < mem_count)
        def _():
            arriving = group_at(step + 1)
            across(arriving).wait_recv()
            pack(arriving)

        work(group_at(step))
        return carry

    lax.fori_loop(0, mem_count, step_work, 0)
    out[0] = out[0] * scale

    for offset in range(1, mem_count):
        across(jnp.int32(offset)).wait_send()
    for number, direction in enumerate(DIRECTIONS):

        @pl.when(present(direction))
        def _():
            for copy in fixed_copies(number, direction):
                copy.wait_send()
            for group in range(mem_count):
                pert_copy(jnp.int32(group), number, direction).wait_send()


def body(mesh_sizes, gradient, perturbations, filter_coef):
    mem_count, lat_count, lon_count = mesh_sizes
    levels, rows, cols = gradient.shape
    per_mem = perturbations.shape[0]
    members = per_mem * mem_count
    assert mem_count & (mem_count - 1) == 0 and HALO * per_mem <= LANES
    assert levels == 1 and rows % 16 == 0 and cols % LANES == 0
    full_rows, full_cols = rows + 2 * HALO, cols + LANES
    packed = (per_mem + 3) // 4 * 2 * SUB
    sizes = (mem_count, lat_count, lon_count, 1.0 / (members - 1))
    return pl.pallas_call(
        functools.partial(kernel, sizes),
        out_shape=jax.ShapeDtypeStruct(gradient.shape, jnp.float32),
        in_specs=[pl.BlockSpec(memory_space=pltpu.HBM)] * 3,
        out_specs=pl.BlockSpec(memory_space=pltpu.VMEM),
        scratch_shapes=[
            pltpu.VMEM((mem_count, per_mem, rows, cols), jnp.bfloat16),
            pltpu.VMEM((per_mem, full_rows, full_cols), jnp.float32),
            pltpu.VMEM((mem_count, 2, packed, cols), jnp.bfloat16),
            pltpu.VMEM((mem_count, 2, rows, LANES), jnp.bfloat16),
            pltpu.VMEM((mem_count, 2, packed, cols + 2 * LANES), jnp.bfloat16),
            pltpu.VMEM((mem_count, 2, rows, LANES), jnp.bfloat16),
            pltpu.VMEM((6, rows + 2 * SUB, cols + 2 * LANES), jnp.float32),
            pltpu.VMEM((9, full_rows, full_cols), jnp.float32),
            pltpu.VMEM((2, full_rows, full_cols), jnp.float32),
            pltpu.SemaphoreType.DMA((mem_count,)),
            pltpu.SemaphoreType.DMA((mem_count,)),
            pltpu.SemaphoreType.DMA((2 + mem_count, len(DIRECTIONS))),
            pltpu.SemaphoreType.DMA((2 + mem_count, len(DIRECTIONS))),
            pltpu.SemaphoreType.DMA((3,)),
        ],
        compiler_params=pltpu.CompilerParams(
            collective_id=0, has_side_effects=True, vmem_limit_bytes=32 * 1024 * 1024
        ),
    )(perturbations, gradient, filter_coef)


def solution(mesh):
    sizes = tuple(mesh.shape[name] for name in ("mem", "lat", "lon"))
    return jax.shard_map(
        functools.partial(body, sizes),
        mesh=mesh,
        in_specs=(P("mem", "lat", "lon"), P("mem", None, "lat", "lon"), P(None, "lat", "lon")),
        out_specs=P("mem", "lat", "lon"),
        check_vma=False,
    )
```

```python
import functools

import jax
import jax.numpy as jnp
from jax import lax
from jax.experimental import pallas as pl
from jax.experimental.pallas import tpu as pltpu
from jax.sharding import PartitionSpec as P

HALO = 4
LANES = 128
SUB = 8
DIRECTIONS = ((-1, 0), (1, 0), (0, -1), (0, 1), (-1, -1), (-1, 1), (1, -1), (1, 1))


def shifted(values, offset, axis):
    return pltpu.roll(values, (-offset) % values.shape[axis], axis)


def circular(centre_rows, north_rows, south_rows, row_low):
    return jnp.concatenate([centre_rows, jnp.where(row_low, south_rows, north_rows)], axis=0)


def folded(padded, cols):
    low = lax.broadcasted_iota(jnp.int32, (padded.shape[0], LANES), 1) < LANES // 2
    side = jnp.where(low, padded[:, LANES + cols :], padded[:, :LANES])
    return jnp.concatenate([padded[:, LANES : LANES + cols], side], axis=1)


def kernel(
    sizes,
    pert,
    grad,
    coef,
    out,
    centre,
    field,
    send_rows,
    send_cols,
    recv_rows,
    recv_cols,
    ext,
    stencils,
    scaled,
    grads,
    sums,
    z_send,
    z_recv,
    sum_send,
    sum_recv,
    grad_send,
    grad_recv,
    halo_send,
    halo_recv,
    local_sem,
):
    mem_count, lat_count, lon_count, scale = sizes
    per_mem, _, rows, cols = pert.shape
    mem, lat, lon = (lax.axis_index(name) for name in ("mem", "lat", "lon"))
    mesh_id = pl.DeviceIdType.MESH

    def present(direction):
        up, right = direction
        checks = []
        if up:
            checks.append(lat > 0 if up < 0 else lat < lat_count - 1)
        if right:
            checks.append(lon > 0 if right < 0 else lon < lon_count - 1)
        return functools.reduce(jnp.logical_and, checks)

    def neighbour(direction):
        return (mem, lat + direction[0], lon + direction[1])

    def peer(offset):
        total, bit = 0, 1
        while bit < mem_count:
            total = total + bit * lax.rem(lax.div(mem, bit) + lax.div(offset, bit), 2)
            bit *= 2
        return total

    def group_at(step):
        return lax.rem(step + 1, mem_count)

    barrier = pltpu.get_barrier_semaphore()
    for offset in range(1, mem_count):
        pl.semaphore_signal(barrier, inc=1, device_id=(peer(jnp.int32(offset)), lat, lon), device_id_type=mesh_id)
    for direction in DIRECTIONS:

        @pl.when(present(direction))
        def _():
            pl.semaphore_signal(barrier, inc=1, device_id=neighbour(direction), device_id_type=mesh_id)

    inner_rows, inner_cols = pl.ds(SUB, rows), pl.ds(LANES, cols)

    def own_pert(group):
        return pltpu.make_async_copy(pert.at[:, peer(group)], centre.at[group], local_sem.at[2 + group])

    own_grad = pltpu.make_async_copy(
        grad.at[0], grads.at[0, inner_rows, inner_cols], local_sem.at[0]
    )
    own_coef = pltpu.make_async_copy(
        coef, ext.at[:, inner_rows, inner_cols], local_sem.at[1]
    )
    for step in range(mem_count):
        own_pert(group_at(jnp.int32(step))).start()
    own_grad.start()
    own_coef.start()

    blocks = [
        1 + jnp.where(here > 0, 1, 0) + jnp.where(here < count - 1, 1, 0)
        for here, count in ((lat, lat_count), (lon, lon_count))
    ]
    pl.semaphore_wait(barrier, mem_count - 2 + blocks[0] * blocks[1])

    def across(offset):
        return pltpu.make_async_remote_copy(
            src_ref=grad.at[0],
            dst_ref=grads.at[offset, inner_rows, inner_cols],
            send_sem=z_send.at[offset],
            recv_sem=z_recv.at[offset],
            device_id=(peer(offset), lat, lon),
            device_id_type=mesh_id,
        )

    def back(offset):
        return pltpu.make_async_remote_copy(
            src_ref=sums.at[0, offset],
            dst_ref=sums.at[1, offset],
            send_sem=sum_send.at[offset],
            recv_sem=sum_recv.at[offset],
            device_id=(peer(offset), lat, lon),
            device_id_type=mesh_id,
        )

    for offset in range(1, mem_count):
        across(jnp.int32(offset)).start()

    def span(step, low, size, edge):
        if step == 0:
            return pl.ds(0, size), pl.ds(low, size)
        if step < 0:
            return pl.ds(0, edge), pl.ds(low + size, edge)
        return pl.ds(size - edge, edge), pl.ds(low - edge, edge)

    def coef_copy(number, direction):
        source_rows, target_rows = span(direction[0], SUB, rows, SUB)
        source_cols, target_cols = span(direction[1], LANES, cols, LANES)
        return pltpu.make_async_remote_copy(
            src_ref=coef.at[:, source_rows, source_cols],
            dst_ref=ext.at[:, target_rows, target_cols],
            send_sem=halo_send.at[mem_count, number],
            recv_sem=halo_recv.at[mem_count, number],
            device_id=neighbour(direction),
            device_id_type=mesh_id,
        )

    def grad_copy(group, number, direction):
        source_rows, target_rows = span(direction[0], SUB, rows, SUB)
        source_cols, target_cols = span(direction[1], LANES, cols, LANES)
        source_rows = pl.ds(source_rows.start + SUB, source_rows.size)
        source_cols = pl.ds(source_cols.start + LANES, source_cols.size)
        return pltpu.make_async_remote_copy(
            src_ref=grads.at[group, source_rows, source_cols],
            dst_ref=grads.at[group, target_rows, target_cols],
            send_sem=grad_send.at[group, number],
            recv_sem=grad_recv.at[group, number],
            device_id=neighbour(direction),
            device_id_type=mesh_id,
        )

    def for_targets(action):
        for number, direction in enumerate(DIRECTIONS):

            @pl.when(present(direction))
            def _():
                action(number, direction)

    def for_sources(action):
        for number, direction in enumerate(DIRECTIONS):

            @pl.when(present((-direction[0], -direction[1])))
            def _():
                action(number, direction)

    def pert_copy(group, number, direction):
        up, right = direction
        if up == 0:
            side = 0 if right < 0 else 1
            source, target = send_cols.at[group, side], recv_cols.at[group, side]
        else:
            side = 0 if up < 0 else 1
            source_cols, target_cols = span(right, LANES, cols, LANES)
            source = send_rows.at[group, side, :, source_cols]
            target = recv_rows.at[group, side, :, target_cols]
        return pltpu.make_async_remote_copy(
            src_ref=source,
            dst_ref=target,
            send_sem=halo_send.at[group, number],
            recv_sem=halo_recv.at[group, number],
            device_id=neighbour(direction),
            device_id_type=mesh_id,
        )

    for_targets(lambda number, direction: coef_copy(number, direction).start())

    low_row = lax.broadcasted_iota(jnp.int32, (SUB, cols), 0) < HALO
    lane = lax.broadcasted_iota(jnp.int32, (rows, LANES), 1)
    tiles = send_rows.shape[2] // SUB

    def pack(group):
        tops, bottoms = [], []
        west = east = None
        for k in range(per_mem):
            block = centre[group, k].astype(jnp.float32)
            top, bottom = block[:SUB], block[rows - SUB :]
            if k % 2:
                tops[-1] = jnp.where(low_row, tops[-1], pltpu.roll(top, HALO, 0))
                bottoms[-1] = jnp.where(low_row, pltpu.roll(bottom, HALO, 0), bottoms[-1])
            else:
                tops.append(top)
                bottoms.append(bottom)
            place = (lane >= HALO * k) & (lane < HALO * (k + 1))
            first = pltpu.roll(block[:, :LANES], HALO * k, 1) if k else block[:, :LANES]
            last = pltpu.roll(block[:, cols - LANES :], HALO * (k + 1) % LANES, 1)
            west = first if west is None else jnp.where(place, first, west)
            east = last if east is None else jnp.where(place, last, east)
        while len(tops) < tiles:
            tops.append(tops[-1])
            bottoms.append(bottoms[-1])
        send_rows[group, 0] = jnp.concatenate(tops, axis=0).astype(jnp.bfloat16)
        send_rows[group, 1] = jnp.concatenate(bottoms, axis=0).astype(jnp.bfloat16)
        send_cols[group, 0] = west.astype(jnp.bfloat16)
        send_cols[group, 1] = east.astype(jnp.bfloat16)
        for_targets(lambda number, direction: pert_copy(group, number, direction).start())

    def forward(group):
        for_targets(lambda number, direction: grad_copy(group, number, direction).start())

    def pack_step(step, carry):
        group = group_at(step)
        own_pert(group).wait()
        pack(group)
        return carry

    lax.fori_loop(0, mem_count, pack_step, 0)
    own_grad.wait()
    forward(jnp.int32(0))
    own_coef.wait()
    for_sources(lambda number, direction: coef_copy(number, direction).wait_recv())

    full_rows, full_cols = rows + 2 * HALO, cols + LANES
    row_index = lax.broadcasted_iota(jnp.int32, (full_rows, full_cols), 0)
    col_index = lax.broadcasted_iota(jnp.int32, (full_rows, full_cols), 1)
    row_index = jnp.where(row_index < rows + HALO, row_index, row_index - full_rows)
    col_index = jnp.where(col_index < cols + LANES // 2, col_index, col_index - full_cols)
    near = (col_index >= -HALO) & (col_index < cols + HALO)
    row_index = row_index + lat * rows
    col_index = col_index + lon * cols
    inside = (
        near
        & (row_index >= 0)
        & (row_index < rows * lat_count)
        & (col_index >= 0)
        & (col_index < cols * lon_count)
    )
    low_row_full = lax.broadcasted_iota(jnp.int32, (SUB, full_cols), 0) < HALO

    def extended(block):
        wide = folded(block, cols)
        wide = circular(
            wide[SUB : SUB + rows], wide[:SUB], wide[SUB + rows :], low_row_full
        )
        return jnp.where(inside, wide, 0.0)

    c0, cn, cs, cw, ce = (extended(ext[index]) for index in range(5))
    for index, value in enumerate((c0, cn, cs, cw, ce)):
        stencils[index] = value
    for index, value in enumerate(
        (shifted(cs, -1, 0), shifted(cn, 1, 0), shifted(ce, -1, 1), shifted(cw, 1, 1))
    ):
        stencils[5 + index] = jnp.where(inside, value, 0.0)
    scaled[1] = inside.astype(jnp.float32)

    def one_pass(values, first):
        total = stencils[0] * values + stencils[first] * shifted(values, -1, 0)
        total = total + stencils[first + 1] * shifted(values, 1, 0)
        total = total + stencils[first + 2] * shifted(values, -1, 1)
        return total + stencils[first + 3] * shifted(values, 1, 1)

    def work(group):
        for_sources(lambda number, direction: pert_copy(group, number, direction).wait_recv())
        for_sources(lambda number, direction: grad_copy(group, number, direction).wait_recv())
        scaled[0] = extended(grads[group])
        total = jnp.zeros((rows, cols), jnp.float32)
        south = folded(recv_rows[group, 0].astype(jnp.float32), cols)
        north = folded(recv_rows[group, 1].astype(jnp.float32), cols)
        from_east = recv_cols[group, 0].astype(jnp.float32)
        from_west = recv_cols[group, 1].astype(jnp.float32)
        for k in range(per_mem):
            block = centre[group, k].astype(jnp.float32)
            tile = slice((k // 2) * SUB, (k // 2 + 1) * SUB)
            south_rows, north_rows = south[tile], north[tile]
            if k % 2:
                south_rows = pltpu.roll(south_rows, HALO, 0)
                north_rows = pltpu.roll(north_rows, HALO, 0)
            east = pltpu.roll(from_east, LANES - HALO * k, 1) if k else from_east
            west = pltpu.roll(from_west, (-HALO * (k + 1)) % LANES, 1)
            side = jnp.where(lane < LANES // 2, east, west)
            field[k] = circular(
                jnp.concatenate([block, side], axis=1), north_rows, south_rows, low_row_full
            )
        for k in range(per_mem):
            values = jnp.where(scaled[1] > 0.5, field[k] * scaled[0], 0.0)
            values = one_pass(values, 5)
            values = one_pass(values, 5)
            values = one_pass(values, 1)
            values = one_pass(values, 1)
            total = total + values[:rows, :cols] * field[k, :rows, :cols]
        sums[0, group] = total

    if mem_count > 1:
        across(jnp.int32(1)).wait_recv()
        forward(jnp.int32(1))

    def step_work(step, carry):
        @pl.when(step + 2 < mem_count)
        def _():
            across(step + 2).wait_recv()
            forward(step + 2)

        group = group_at(step)
        work(group)

        @pl.when(step + 1 < mem_count)
        def _():
            back(group).start()

        return carry

    lax.fori_loop(0, mem_count, step_work, 0)
    total = sums[0, 0]
    for offset in range(1, mem_count):
        back(jnp.int32(offset)).wait_recv()
        total = total + sums[1, offset]
    out[0] = total * scale

    for offset in range(1, mem_count):
        across(jnp.int32(offset)).wait_send()
        back(jnp.int32(offset)).wait_send()
    for_targets(lambda number, direction: coef_copy(number, direction).wait_send())
    for group in range(mem_count):
        for_targets(lambda number, direction: pert_copy(jnp.int32(group), number, direction).wait_send())
        for_targets(lambda number, direction: grad_copy(jnp.int32(group), number, direction).wait_send())


def body(mesh_sizes, gradient, perturbations, filter_coef):
    mem_count, lat_count, lon_count = mesh_sizes
    levels, rows, cols = gradient.shape
    per_mem = perturbations.shape[0]
    members = per_mem * mem_count
    assert mem_count & (mem_count - 1) == 0 and HALO * per_mem <= LANES
    assert levels == 1 and rows % 16 == 0 and cols % LANES == 0
    full_rows, full_cols = rows + 2 * HALO, cols + LANES
    packed = (per_mem + 3) // 4 * 2 * SUB
    sizes = (mem_count, lat_count, lon_count, 1.0 / (members - 1))
    return pl.pallas_call(
        functools.partial(kernel, sizes),
        out_shape=jax.ShapeDtypeStruct(gradient.shape, jnp.float32),
        in_specs=[pl.BlockSpec(memory_space=pltpu.HBM)] * 3,
        out_specs=pl.BlockSpec(memory_space=pltpu.VMEM),
        scratch_shapes=[
            pltpu.VMEM((mem_count, per_mem, rows, cols), jnp.bfloat16),
            pltpu.VMEM((per_mem, full_rows, full_cols), jnp.float32),
            pltpu.VMEM((mem_count, 2, packed, cols), jnp.bfloat16),
            pltpu.VMEM((mem_count, 2, rows, LANES), jnp.bfloat16),
            pltpu.VMEM((mem_count, 2, packed, cols + 2 * LANES), jnp.bfloat16),
            pltpu.VMEM((mem_count, 2, rows, LANES), jnp.bfloat16),
            pltpu.VMEM((5, rows + 2 * SUB, cols + 2 * LANES), jnp.float32),
            pltpu.VMEM((9, full_rows, full_cols), jnp.float32),
            pltpu.VMEM((2, full_rows, full_cols), jnp.float32),
            pltpu.VMEM((mem_count, rows + 2 * SUB, cols + 2 * LANES), jnp.float32),
            pltpu.VMEM((2, mem_count, rows, cols), jnp.float32),
            pltpu.SemaphoreType.DMA((mem_count,)),
            pltpu.SemaphoreType.DMA((mem_count,)),
            pltpu.SemaphoreType.DMA((mem_count,)),
            pltpu.SemaphoreType.DMA((mem_count,)),
            pltpu.SemaphoreType.DMA((mem_count, len(DIRECTIONS))),
            pltpu.SemaphoreType.DMA((mem_count, len(DIRECTIONS))),
            pltpu.SemaphoreType.DMA((mem_count + 1, len(DIRECTIONS))),
            pltpu.SemaphoreType.DMA((mem_count + 1, len(DIRECTIONS))),
            pltpu.SemaphoreType.DMA((2 + mem_count,)),
        ],
        compiler_params=pltpu.CompilerParams(
            collective_id=0, has_side_effects=True, vmem_limit_bytes=60 * 1024 * 1024
        ),
    )(perturbations, gradient, filter_coef)


def solution(mesh):
    sizes = tuple(mesh.shape[name] for name in ("mem", "lat", "lon"))
    return jax.shard_map(
        functools.partial(body, sizes),
        mesh=mesh,
        in_specs=(P("mem", "lat", "lon"), P("mem", None, "lat", "lon"), P(None, "lat", "lon")),
        out_specs=P("mem", "lat", "lon"),
        check_vma=False,
    )
```

```python
import functools

import jax
import jax.numpy as jnp
from jax import lax
from jax.experimental import pallas as pl
from jax.experimental.pallas import tpu as pltpu
from jax.sharding import PartitionSpec as P

HALO = 4
LANES = 128
SUB = 8
DIRECTIONS = ((-1, 0), (1, 0), (0, -1), (0, 1), (-1, -1), (-1, 1), (1, -1), (1, 1))


def shifted(values, offset, axis):
    unit = (SUB, LANES)[axis]
    size = values.shape[axis]
    if offset < 0:
        edge = pltpu.roll(lax.slice_in_dim(values, size - unit, size, axis=axis), 1, axis)
        return jnp.concatenate([edge, lax.slice_in_dim(values, 0, size - unit, axis=axis)], axis=axis)
    edge = pltpu.roll(lax.slice_in_dim(values, 0, unit, axis=axis), unit - 1, axis)
    return jnp.concatenate([lax.slice_in_dim(values, unit, size, axis=axis), edge], axis=axis)


def place_of(index, unit, size):
    return (index % unit) * (size // unit) + index // unit


def ones_where(condition):
    return jnp.where(condition, 1.0, 0.0).astype(jnp.bfloat16)


def iotas(shape):
    return [lax.broadcasted_iota(jnp.int32, shape, axis) for axis in range(2)]


def parts_of(values):
    high = values.astype(jnp.bfloat16).astype(jnp.float32)
    rest = values - high
    middle = rest.astype(jnp.bfloat16).astype(jnp.float32)
    return jnp.concatenate(
        [high, middle, rest - middle, jnp.zeros((SUB, values.shape[1]), jnp.float32)], axis=0
    ).astype(jnp.bfloat16)


def product(left, right):
    return jnp.dot(left, right, preferred_element_type=jnp.float32)


def circular(centre_rows, north_rows, south_rows, row_low):
    return jnp.concatenate([centre_rows, jnp.where(row_low, south_rows, north_rows)], axis=0)


def folded(padded, cols):
    low = lax.broadcasted_iota(jnp.int32, (padded.shape[0], LANES), 1) < LANES // 2
    side = jnp.where(low, padded[:, LANES + cols :], padded[:, :LANES])
    return jnp.concatenate([padded[:, LANES : LANES + cols], side], axis=1)


def kernel(
    sizes,
    pert,
    grad,
    coef,
    out,
    centre,
    field,
    send_rows,
    send_cols,
    recv_rows,
    recv_cols,
    ext,
    stencils,
    scaled,
    grads,
    sums,
    perm_cols,
    perm_rows,
    perm_parts,
    back_cols,
    back_parts,
    z_send,
    z_recv,
    sum_send,
    sum_recv,
    grad_send,
    grad_recv,
    halo_send,
    halo_recv,
    local_sem,
):
    mem_count, lat_count, lon_count, scale = sizes
    per_mem, _, rows, cols = pert.shape
    mem, lat, lon = (lax.axis_index(name) for name in ("mem", "lat", "lon"))
    mesh_id = pl.DeviceIdType.MESH

    def present(direction):
        up, right = direction
        checks = []
        if up:
            checks.append(lat > 0 if up < 0 else lat < lat_count - 1)
        if right:
            checks.append(lon > 0 if right < 0 else lon < lon_count - 1)
        return functools.reduce(jnp.logical_and, checks)

    def neighbour(direction):
        return (mem, lat + direction[0], lon + direction[1])

    def peer(offset):
        total, bit = 0, 1
        while bit < mem_count:
            total = total + bit * lax.rem(lax.div(mem, bit) + lax.div(offset, bit), 2)
            bit *= 2
        return total

    def group_at(step):
        return lax.rem(step + 1, mem_count)

    barrier = pltpu.get_barrier_semaphore()
    for offset in range(1, mem_count):
        pl.semaphore_signal(barrier, inc=1, device_id=(peer(jnp.int32(offset)), lat, lon), device_id_type=mesh_id)
    for direction in DIRECTIONS:

        @pl.when(present(direction))
        def _():
            pl.semaphore_signal(barrier, inc=1, device_id=neighbour(direction), device_id_type=mesh_id)

    inner_rows, inner_cols = pl.ds(SUB, rows), pl.ds(LANES, cols)

    def own_pert(group):
        return pltpu.make_async_copy(pert.at[:, peer(group)], centre.at[group], local_sem.at[2 + group])

    own_grad = pltpu.make_async_copy(
        grad.at[0], grads.at[0, inner_rows, inner_cols], local_sem.at[0]
    )
    own_coef = pltpu.make_async_copy(
        coef, ext.at[:, inner_rows, inner_cols], local_sem.at[1]
    )
    for step in range(mem_count):
        own_pert(group_at(jnp.int32(step))).start()
    own_grad.start()
    own_coef.start()

    blocks = [
        1 + jnp.where(here > 0, 1, 0) + jnp.where(here < count - 1, 1, 0)
        for here, count in ((lat, lat_count), (lon, lon_count))
    ]
    pl.semaphore_wait(barrier, mem_count - 2 + blocks[0] * blocks[1])

    def across(offset):
        return pltpu.make_async_remote_copy(
            src_ref=grad.at[0],
            dst_ref=grads.at[offset, inner_rows, inner_cols],
            send_sem=z_send.at[offset],
            recv_sem=z_recv.at[offset],
            device_id=(peer(offset), lat, lon),
            device_id_type=mesh_id,
        )

    def back(offset):
        return pltpu.make_async_remote_copy(
            src_ref=sums.at[0, offset],
            dst_ref=sums.at[1, offset],
            send_sem=sum_send.at[offset],
            recv_sem=sum_recv.at[offset],
            device_id=(peer(offset), lat, lon),
            device_id_type=mesh_id,
        )

    for offset in range(1, mem_count):
        across(jnp.int32(offset)).start()

    def span(step, low, size, edge):
        if step == 0:
            return pl.ds(0, size), pl.ds(low, size)
        if step < 0:
            return pl.ds(0, edge), pl.ds(low + size, edge)
        return pl.ds(size - edge, edge), pl.ds(low - edge, edge)

    def coef_copy(number, direction):
        source_rows, target_rows = span(direction[0], SUB, rows, SUB)
        source_cols, target_cols = span(direction[1], LANES, cols, LANES)
        return pltpu.make_async_remote_copy(
            src_ref=coef.at[:, source_rows, source_cols],
            dst_ref=ext.at[:, target_rows, target_cols],
            send_sem=halo_send.at[mem_count, number],
            recv_sem=halo_recv.at[mem_count, number],
            device_id=neighbour(direction),
            device_id_type=mesh_id,
        )

    def grad_copy(group, number, direction):
        source_rows, target_rows = span(direction[0], SUB, rows, SUB)
        source_cols, target_cols = span(direction[1], LANES, cols, LANES)
        source_rows = pl.ds(source_rows.start + SUB, source_rows.size)
        source_cols = pl.ds(source_cols.start + LANES, source_cols.size)
        return pltpu.make_async_remote_copy(
            src_ref=grads.at[group, source_rows, source_cols],
            dst_ref=grads.at[group, target_rows, target_cols],
            send_sem=grad_send.at[group, number],
            recv_sem=grad_recv.at[group, number],
            device_id=neighbour(direction),
            device_id_type=mesh_id,
        )

    def for_targets(action):
        for number, direction in enumerate(DIRECTIONS):

            @pl.when(present(direction))
            def _():
                action(number, direction)

    def for_sources(action):
        for number, direction in enumerate(DIRECTIONS):

            @pl.when(present((-direction[0], -direction[1])))
            def _():
                action(number, direction)

    def pert_copy(group, number, direction):
        up, right = direction
        if up == 0:
            side = 0 if right < 0 else 1
            source, target = send_cols.at[group, side], recv_cols.at[group, side]
        else:
            side = 0 if up < 0 else 1
            source_cols, target_cols = span(right, LANES, cols, LANES)
            source = send_rows.at[group, side, :, source_cols]
            target = recv_rows.at[group, side, :, target_cols]
        return pltpu.make_async_remote_copy(
            src_ref=source,
            dst_ref=target,
            send_sem=halo_send.at[group, number],
            recv_sem=halo_recv.at[group, number],
            device_id=neighbour(direction),
            device_id_type=mesh_id,
        )

    for_targets(lambda number, direction: coef_copy(number, direction).start())

    low_row = lax.broadcasted_iota(jnp.int32, (SUB, cols), 0) < HALO
    lane = lax.broadcasted_iota(jnp.int32, (rows, LANES), 1)
    tiles = send_rows.shape[2] // SUB

    def pack(group):
        tops, bottoms = [], []
        west = east = None
        for k in range(per_mem):
            block = centre[group, k].astype(jnp.float32)
            top, bottom = block[:SUB], block[rows - SUB :]
            if k % 2:
                tops[-1] = jnp.where(low_row, tops[-1], pltpu.roll(top, HALO, 0))
                bottoms[-1] = jnp.where(low_row, pltpu.roll(bottom, HALO, 0), bottoms[-1])
            else:
                tops.append(top)
                bottoms.append(bottom)
            place = (lane >= HALO * k) & (lane < HALO * (k + 1))
            first = pltpu.roll(block[:, :LANES], HALO * k, 1) if k else block[:, :LANES]
            last = pltpu.roll(block[:, cols - LANES :], HALO * (k + 1) % LANES, 1)
            west = first if west is None else jnp.where(place, first, west)
            east = last if east is None else jnp.where(place, last, east)
        while len(tops) < tiles:
            tops.append(tops[-1])
            bottoms.append(bottoms[-1])
        send_rows[group, 0] = jnp.concatenate(tops, axis=0).astype(jnp.bfloat16)
        send_rows[group, 1] = jnp.concatenate(bottoms, axis=0).astype(jnp.bfloat16)
        send_cols[group, 0] = west.astype(jnp.bfloat16)
        send_cols[group, 1] = east.astype(jnp.bfloat16)
        for_targets(lambda number, direction: pert_copy(group, number, direction).start())

    def forward(group):
        for_targets(lambda number, direction: grad_copy(group, number, direction).start())

    def pack_step(step, carry):
        group = group_at(step)
        own_pert(group).wait()
        pack(group)
        return carry

    lax.fori_loop(0, mem_count, pack_step, 0)
    own_grad.wait()
    forward(jnp.int32(0))
    own_coef.wait()
    for_sources(lambda number, direction: coef_copy(number, direction).wait_recv())

    full_rows, full_cols = rows + 2 * HALO, cols + LANES

    def inside_of(row_index, col_index):
        row_index = jnp.where(row_index < rows + HALO, row_index, row_index - full_rows)
        col_index = jnp.where(col_index < cols + LANES // 2, col_index, col_index - full_cols)
        near = (col_index >= -HALO) & (col_index < cols + HALO)
        row_index = row_index + lat * rows
        col_index = col_index + lon * cols
        return (
            near
            & (row_index >= 0)
            & (row_index < rows * lat_count)
            & (col_index >= 0)
            & (col_index < cols * lon_count)
        )

    row_index, col_index = iotas((full_rows, full_cols))
    inside = inside_of(row_index, col_index)
    inside_here = inside_of(
        place_of(row_index, SUB, full_rows), place_of(col_index, LANES, full_cols)
    )
    scaled[1] = inside.astype(jnp.float32)

    source, target = iotas((full_cols, full_cols))
    perm_cols[...] = ones_where(source == place_of(target, LANES, full_cols))
    source, target = iotas((full_cols, cols))
    back_cols[...] = ones_where(target == place_of(source, LANES, full_cols))
    target, source = iotas(perm_rows.shape)
    perm_rows[...] = ones_where(
        source == target // full_rows * full_rows + place_of(target % full_rows, SUB, full_rows)
    )
    target, source = iotas(perm_parts.shape)
    perm_parts[...] = ones_where(
        (source < 3 * full_rows)
        & (source % full_rows == place_of(target, SUB, full_rows))
    )
    target, source = iotas(back_parts.shape)
    back_parts[...] = ones_where(
        (source < 3 * full_rows)
        & (target == place_of(source % full_rows, SUB, full_rows))
    )
    low_row_full = lax.broadcasted_iota(jnp.int32, (SUB, full_cols), 0) < HALO

    def extended(block):
        wide = folded(block, cols)
        wide = circular(
            wide[SUB : SUB + rows], wide[:SUB], wide[SUB + rows :], low_row_full
        )
        wide = parts_of(jnp.where(scaled[1] > 0.5, wide, 0.0))
        wide = product(wide, perm_cols[...]).astype(jnp.bfloat16)
        return product(perm_parts[...], wide)

    c0, cn, cs, cw, ce = (extended(ext[index]) for index in range(5))
    for index, value in enumerate((c0, cn, cs, cw, ce)):
        stencils[index] = value
    for index, value in enumerate(
        (shifted(cs, -1, 0), shifted(cn, 1, 0), shifted(ce, -1, 1), shifted(cw, 1, 1))
    ):
        stencils[5 + index] = jnp.where(inside_here, value, 0.0)

    def one_pass(values, first):
        total = stencils[0] * values + stencils[first] * shifted(values, -1, 0)
        total = total + stencils[first + 1] * shifted(values, 1, 0)
        total = total + stencils[first + 2] * shifted(values, -1, 1)
        return total + stencils[first + 3] * shifted(values, 1, 1)

    def work(group):
        for_sources(lambda number, direction: pert_copy(group, number, direction).wait_recv())
        for_sources(lambda number, direction: grad_copy(group, number, direction).wait_recv())
        scaled[0] = extended(grads[group])
        total = jnp.zeros((full_rows, full_cols), jnp.float32)
        south = folded(recv_rows[group, 0].astype(jnp.float32), cols)
        north = folded(recv_rows[group, 1].astype(jnp.float32), cols)
        from_east = recv_cols[group, 0].astype(jnp.float32)
        from_west = recv_cols[group, 1].astype(jnp.float32)
        blocks = []
        for k in range(per_mem):
            block = centre[group, k].astype(jnp.float32)
            tile = slice((k // 2) * SUB, (k // 2 + 1) * SUB)
            south_rows, north_rows = south[tile], north[tile]
            if k % 2:
                south_rows = pltpu.roll(south_rows, HALO, 0)
                north_rows = pltpu.roll(north_rows, HALO, 0)
            east = pltpu.roll(from_east, LANES - HALO * k, 1) if k else from_east
            west = pltpu.roll(from_west, (-HALO * (k + 1)) % LANES, 1)
            side = jnp.where(lane < LANES // 2, east, west)
            block = circular(
                jnp.concatenate([block, side], axis=1), north_rows, south_rows, low_row_full
            )
            blocks.append(jnp.where(scaled[1] > 0.5, block, 0.0))
        missing = perm_rows.shape[1] - per_mem * full_rows
        if missing:
            blocks.append(jnp.zeros((missing, full_cols), jnp.float32))
        stack = jnp.concatenate(blocks, axis=0).astype(jnp.bfloat16)
        stack = product(stack, perm_cols[...]).astype(jnp.bfloat16)
        field[...] = product(perm_rows[...], stack)
        for k in range(per_mem):
            here = slice(k * full_rows, (k + 1) * full_rows)
            values = field[here] * scaled[0]
            values = one_pass(values, 5)
            values = one_pass(values, 5)
            values = one_pass(values, 1)
            values = one_pass(values, 1)
            total = total + values * field[here]
        total = product(parts_of(total), back_cols[...]).astype(jnp.bfloat16)
        sums[0, group] = product(back_parts[...], total)

    if mem_count > 1:
        across(jnp.int32(1)).wait_recv()
        forward(jnp.int32(1))

    def step_work(step, carry):
        @pl.when(step + 2 < mem_count)
        def _():
            across(step + 2).wait_recv()
            forward(step + 2)

        group = group_at(step)
        work(group)

        @pl.when(step + 1 < mem_count)
        def _():
            back(group).start()

        return carry

    lax.fori_loop(0, mem_count, step_work, 0)
    total = sums[0, 0]
    for offset in range(1, mem_count):
        back(jnp.int32(offset)).wait_recv()
        total = total + sums[1, offset]
    out[0] = total * scale

    for offset in range(1, mem_count):
        across(jnp.int32(offset)).wait_send()
        back(jnp.int32(offset)).wait_send()
    for_targets(lambda number, direction: coef_copy(number, direction).wait_send())
    for group in range(mem_count):
        for_targets(lambda number, direction: pert_copy(jnp.int32(group), number, direction).wait_send())
        for_targets(lambda number, direction: grad_copy(jnp.int32(group), number, direction).wait_send())


def body(mesh_sizes, gradient, perturbations, filter_coef):
    mem_count, lat_count, lon_count = mesh_sizes
    levels, rows, cols = gradient.shape
    per_mem = perturbations.shape[0]
    members = per_mem * mem_count
    assert mem_count & (mem_count - 1) == 0 and HALO * per_mem <= LANES
    assert levels == 1 and rows % 16 == 0 and cols % LANES == 0
    full_rows, full_cols = rows + 2 * HALO, cols + LANES
    packed = (per_mem + 3) // 4 * 2 * SUB
    sizes = (mem_count, lat_count, lon_count, 1.0 / (members - 1))
    return pl.pallas_call(
        functools.partial(kernel, sizes),
        out_shape=jax.ShapeDtypeStruct(gradient.shape, jnp.float32),
        in_specs=[pl.BlockSpec(memory_space=pltpu.HBM)] * 3,
        out_specs=pl.BlockSpec(memory_space=pltpu.VMEM),
        scratch_shapes=[
            pltpu.VMEM((mem_count, per_mem, rows, cols), jnp.bfloat16),
            pltpu.VMEM((per_mem * full_rows, full_cols), jnp.float32),
            pltpu.VMEM((mem_count, 2, packed, cols), jnp.bfloat16),
            pltpu.VMEM((mem_count, 2, rows, LANES), jnp.bfloat16),
            pltpu.VMEM((mem_count, 2, packed, cols + 2 * LANES), jnp.bfloat16),
            pltpu.VMEM((mem_count, 2, rows, LANES), jnp.bfloat16),
            pltpu.VMEM((5, rows + 2 * SUB, cols + 2 * LANES), jnp.float32),
            pltpu.VMEM((9, full_rows, full_cols), jnp.float32),
            pltpu.VMEM((2, full_rows, full_cols), jnp.float32),
            pltpu.VMEM((mem_count, rows + 2 * SUB, cols + 2 * LANES), jnp.float32),
            pltpu.VMEM((2, mem_count, rows, cols), jnp.float32),
            pltpu.VMEM((full_cols, full_cols), jnp.bfloat16),
            pltpu.VMEM((per_mem * full_rows, -(-per_mem * full_rows // 16) * 16), jnp.bfloat16),
            pltpu.VMEM((full_rows, 3 * full_rows + SUB), jnp.bfloat16),
            pltpu.VMEM((full_cols, cols), jnp.bfloat16),
            pltpu.VMEM((rows, 3 * full_rows + SUB), jnp.bfloat16),
            pltpu.SemaphoreType.DMA((mem_count,)),
            pltpu.SemaphoreType.DMA((mem_count,)),
            pltpu.SemaphoreType.DMA((mem_count,)),
            pltpu.SemaphoreType.DMA((mem_count,)),
            pltpu.SemaphoreType.DMA((mem_count, len(DIRECTIONS))),
            pltpu.SemaphoreType.DMA((mem_count, len(DIRECTIONS))),
            pltpu.SemaphoreType.DMA((mem_count + 1, len(DIRECTIONS))),
            pltpu.SemaphoreType.DMA((mem_count + 1, len(DIRECTIONS))),
            pltpu.SemaphoreType.DMA((2 + mem_count,)),
        ],
        compiler_params=pltpu.CompilerParams(
            collective_id=0, has_side_effects=True, vmem_limit_bytes=60 * 1024 * 1024
        ),
    )(perturbations, gradient, filter_coef)


def solution(mesh):
    sizes = tuple(mesh.shape[name] for name in ("mem", "lat", "lon"))
    return jax.shard_map(
        functools.partial(body, sizes),
        mesh=mesh,
        in_specs=(P("mem", "lat", "lon"), P("mem", None, "lat", "lon"), P(None, "lat", "lon")),
        out_specs=P("mem", "lat", "lon"),
        check_vma=False,
    )
```

```python
import functools

import jax
import jax.numpy as jnp
from jax import lax
from jax.experimental import pallas as pl
from jax.experimental.pallas import tpu as pltpu
from jax.sharding import PartitionSpec as P

HALO = 4
LANES = 128
SUB = 8
DIRECTIONS = ((-1, 0), (1, 0), (0, -1), (0, 1), (-1, -1), (-1, 1), (1, -1), (1, 1))


def shifted(values, offset, axis):
    unit = (SUB, LANES)[axis]
    size = values.shape[axis]
    if offset < 0:
        edge = pltpu.roll(lax.slice_in_dim(values, size - unit, size, axis=axis), 1, axis)
        return jnp.concatenate([edge, lax.slice_in_dim(values, 0, size - unit, axis=axis)], axis=axis)
    edge = pltpu.roll(lax.slice_in_dim(values, 0, unit, axis=axis), unit - 1, axis)
    return jnp.concatenate([lax.slice_in_dim(values, unit, size, axis=axis), edge], axis=axis)


def place_of(index, unit, size):
    return (index % unit) * (size // unit) + index // unit


def ones_where(condition):
    return jnp.where(condition, 1.0, 0.0).astype(jnp.bfloat16)


def iotas(shape):
    return [lax.broadcasted_iota(jnp.int32, shape, axis) for axis in range(2)]


def parts_of(values):
    high = values.astype(jnp.bfloat16).astype(jnp.float32)
    rest = values - high
    middle = rest.astype(jnp.bfloat16).astype(jnp.float32)
    return jnp.concatenate(
        [high, middle, rest - middle, jnp.zeros((SUB, values.shape[1]), jnp.float32)], axis=0
    ).astype(jnp.bfloat16)


def product(left, right):
    return jnp.dot(left, right, preferred_element_type=jnp.float32)


def circular(centre_rows, north_rows, south_rows, row_low):
    return jnp.concatenate([centre_rows, jnp.where(row_low, south_rows, north_rows)], axis=0)


def folded(padded, cols):
    low = lax.broadcasted_iota(jnp.int32, (padded.shape[0], LANES), 1) < LANES // 2
    side = jnp.where(low, padded[:, LANES + cols :], padded[:, :LANES])
    return jnp.concatenate([padded[:, LANES : LANES + cols], side], axis=1)


def kernel(
    sizes,
    pert,
    grad,
    coef,
    out,
    centre,
    field,
    send_rows,
    send_cols,
    recv_rows,
    recv_cols,
    ext,
    stencils,
    scaled,
    grads,
    sums,
    perm_cols,
    perm_rows,
    perm_parts,
    back_cols,
    back_parts,
    z_send,
    z_recv,
    sum_send,
    sum_recv,
    halo_send,
    halo_recv,
    local_sem,
):
    mem_count, lat_count, lon_count, scale = sizes
    per_mem, _, rows, cols = pert.shape
    mem, lat, lon = (lax.axis_index(name) for name in ("mem", "lat", "lon"))
    mesh_id = pl.DeviceIdType.MESH

    def present(direction):
        up, right = direction
        checks = []
        if up:
            checks.append(lat > 0 if up < 0 else lat < lat_count - 1)
        if right:
            checks.append(lon > 0 if right < 0 else lon < lon_count - 1)
        return functools.reduce(jnp.logical_and, checks)

    def neighbour(direction):
        return (mem, lat + direction[0], lon + direction[1])

    def peer(offset):
        total, bit = 0, 1
        while bit < mem_count:
            total = total + bit * lax.rem(lax.div(mem, bit) + lax.div(offset, bit), 2)
            bit *= 2
        return total

    def group_at(step):
        return lax.rem(step + 1, mem_count)

    barrier = pltpu.get_barrier_semaphore()
    for offset in range(1, mem_count):
        pl.semaphore_signal(barrier, inc=1, device_id=(peer(jnp.int32(offset)), lat, lon), device_id_type=mesh_id)
    for direction in DIRECTIONS:

        @pl.when(present(direction))
        def _():
            pl.semaphore_signal(barrier, inc=1, device_id=neighbour(direction), device_id_type=mesh_id)

    inner_rows, inner_cols = pl.ds(SUB, rows), pl.ds(LANES, cols)

    own_pert = pltpu.make_async_copy(pert, centre, local_sem.at[2])
    own_grad = pltpu.make_async_copy(
        grad.at[0], grads.at[0, inner_rows, inner_cols], local_sem.at[0]
    )
    own_coef = pltpu.make_async_copy(
        coef, ext.at[:, inner_rows, inner_cols], local_sem.at[1]
    )
    own_pert.start()
    own_grad.start()
    own_coef.start()

    full_rows, full_cols = rows + 2 * HALO, cols + LANES

    def inside_of(row_index, col_index):
        row_index = jnp.where(row_index < rows + HALO, row_index, row_index - full_rows)
        col_index = jnp.where(col_index < cols + LANES // 2, col_index, col_index - full_cols)
        near = (col_index >= -HALO) & (col_index < cols + HALO)
        row_index = row_index + lat * rows
        col_index = col_index + lon * cols
        return (
            near
            & (row_index >= 0)
            & (row_index < rows * lat_count)
            & (col_index >= 0)
            & (col_index < cols * lon_count)
        )

    def line(size, axis):
        return lax.broadcasted_iota(jnp.int32, (size, 1) if axis == 0 else (1, size), axis)

    inside = inside_of(*iotas((full_rows, full_cols)))
    scaled[1] = inside.astype(jnp.float32)
    inside_here = inside_of(
        place_of(line(full_rows, 0), SUB, full_rows), place_of(line(full_cols, 1), LANES, full_cols)
    )

    def sized(ref, axis):
        return line(ref.shape[axis], axis)

    place = place_of(sized(perm_cols, 1), LANES, full_cols)
    perm_cols[...] = ones_where(iotas(perm_cols.shape)[0] == place)
    place = place_of(sized(back_cols, 0), LANES, full_cols)
    back_cols[...] = ones_where(iotas(back_cols.shape)[1] == place)
    target = sized(perm_rows, 0)
    place = target // full_rows * full_rows + place_of(target % full_rows, SUB, full_rows)
    perm_rows[...] = ones_where(iotas(perm_rows.shape)[1] == place)
    source = sized(perm_parts, 1)
    source = jnp.where(source < 3 * full_rows, source % full_rows, -1)
    place = place_of(sized(perm_parts, 0), SUB, full_rows)
    perm_parts[...] = ones_where(source == place)
    source = sized(back_parts, 1)
    place = place_of(source % full_rows, SUB, full_rows)
    place = jnp.where(source < 3 * full_rows, place, -1)
    back_parts[...] = ones_where(iotas(back_parts.shape)[0] == place)
    low_row_full = lax.broadcasted_iota(jnp.int32, (SUB, full_cols), 0) < HALO

    blocks = [
        1 + jnp.where(here > 0, 1, 0) + jnp.where(here < count - 1, 1, 0)
        for here, count in ((lat, lat_count), (lon, lon_count))
    ]
    pl.semaphore_wait(barrier, mem_count - 2 + blocks[0] * blocks[1])

    def across(offset):
        return pltpu.make_async_remote_copy(
            src_ref=grad.at[0],
            dst_ref=grads.at[offset, inner_rows, inner_cols],
            send_sem=z_send.at[offset],
            recv_sem=z_recv.at[offset],
            device_id=(peer(offset), lat, lon),
            device_id_type=mesh_id,
        )

    def back(offset):
        return pltpu.make_async_remote_copy(
            src_ref=sums.at[0, offset],
            dst_ref=sums.at[1, offset],
            send_sem=sum_send.at[offset],
            recv_sem=sum_recv.at[offset],
            device_id=(peer(offset), lat, lon),
            device_id_type=mesh_id,
        )

    for offset in range(1, mem_count):
        across(jnp.int32(offset)).start()

    def span(step, low, size, edge):
        if step == 0:
            return pl.ds(0, size), pl.ds(low, size)
        if step < 0:
            return pl.ds(0, edge), pl.ds(low + size, edge)
        return pl.ds(size - edge, edge), pl.ds(low - edge, edge)

    def coef_copy(number, direction):
        source_rows, target_rows = span(direction[0], SUB, rows, SUB)
        source_cols, target_cols = span(direction[1], LANES, cols, LANES)
        return pltpu.make_async_remote_copy(
            src_ref=coef.at[:, source_rows, source_cols],
            dst_ref=ext.at[:, target_rows, target_cols],
            send_sem=halo_send.at[0, number],
            recv_sem=halo_recv.at[0, number],
            device_id=neighbour(direction),
            device_id_type=mesh_id,
        )

    def grad_copy(number, direction):
        source_rows, target_rows = span(direction[0], SUB, rows, SUB)
        source_cols, target_cols = span(direction[1], LANES, cols, LANES)
        source_rows = pl.ds(source_rows.start + SUB, source_rows.size)
        source_cols = pl.ds(source_cols.start + LANES, source_cols.size)
        return pltpu.make_async_remote_copy(
            src_ref=grads.at[:, source_rows, source_cols],
            dst_ref=grads.at[:, target_rows, target_cols],
            send_sem=halo_send.at[1, number],
            recv_sem=halo_recv.at[1, number],
            device_id=neighbour(direction),
            device_id_type=mesh_id,
        )

    def pert_copy(number, direction):
        up, right = direction
        if up == 0:
            side = 0 if right < 0 else 1
            source, target = send_cols.at[side], recv_cols.at[side]
        else:
            side = 0 if up < 0 else 1
            source_cols, target_cols = span(right, LANES, cols, LANES)
            source = send_rows.at[side, :, :, source_cols]
            target = recv_rows.at[side, :, :, target_cols]
        return pltpu.make_async_remote_copy(
            src_ref=source,
            dst_ref=target,
            send_sem=halo_send.at[2, number],
            recv_sem=halo_recv.at[2, number],
            device_id=neighbour(direction),
            device_id_type=mesh_id,
        )

    def for_targets(action):
        for number, direction in enumerate(DIRECTIONS):

            @pl.when(present(direction))
            def _():
                action(number, direction)

    def for_sources(action):
        for number, direction in enumerate(DIRECTIONS):

            @pl.when(present((-direction[0], -direction[1])))
            def _():
                action(number, direction)

    for_targets(lambda number, direction: coef_copy(number, direction).start())

    low_row = lax.broadcasted_iota(jnp.int32, (SUB, cols), 0) < HALO
    lane = lax.broadcasted_iota(jnp.int32, (rows, LANES), 1)
    tiles = send_rows.shape[2] // SUB

    def pack(group, carry):
        tops, bottoms = [], []
        west = east = None
        for k in range(per_mem):
            block = centre[k, peer(group)].astype(jnp.float32)
            top, bottom = block[:SUB], block[rows - SUB :]
            if k % 2:
                tops[-1] = jnp.where(low_row, tops[-1], pltpu.roll(top, HALO, 0))
                bottoms[-1] = jnp.where(low_row, pltpu.roll(bottom, HALO, 0), bottoms[-1])
            else:
                tops.append(top)
                bottoms.append(bottom)
            place = (lane >= HALO * k) & (lane < HALO * (k + 1))
            first = pltpu.roll(block[:, :LANES], HALO * k, 1) if k else block[:, :LANES]
            last = pltpu.roll(block[:, cols - LANES :], HALO * (k + 1) % LANES, 1)
            west = first if west is None else jnp.where(place, first, west)
            east = last if east is None else jnp.where(place, last, east)
        while len(tops) < tiles:
            tops.append(tops[-1])
            bottoms.append(bottoms[-1])
        send_rows[0, group] = jnp.concatenate(tops, axis=0).astype(jnp.bfloat16)
        send_rows[1, group] = jnp.concatenate(bottoms, axis=0).astype(jnp.bfloat16)
        send_cols[0, group] = west.astype(jnp.bfloat16)
        send_cols[1, group] = east.astype(jnp.bfloat16)
        return carry

    own_pert.wait()
    lax.fori_loop(0, mem_count, pack, 0)
    for_targets(lambda number, direction: pert_copy(number, direction).start())
    own_coef.wait()
    for_sources(lambda number, direction: coef_copy(number, direction).wait_recv())

    def extended(block):
        wide = folded(block, cols)
        wide = circular(
            wide[SUB : SUB + rows], wide[:SUB], wide[SUB + rows :], low_row_full
        )
        wide = parts_of(jnp.where(scaled[1] > 0.5, wide, 0.0))
        wide = product(wide, perm_cols[...]).astype(jnp.bfloat16)
        return product(perm_parts[...], wide)

    c0, cn, cs, cw, ce = (extended(ext[index]) for index in range(5))
    for index, value in enumerate((c0, cn, cs, cw, ce)):
        stencils[index] = value
    for index, value in enumerate(
        (shifted(cs, -1, 0), shifted(cn, 1, 0), shifted(ce, -1, 1), shifted(cw, 1, 1))
    ):
        stencils[5 + index] = jnp.where(inside_here, value, 0.0)

    def one_pass(values, first):
        total = stencils[0] * values + stencils[first] * shifted(values, -1, 0)
        total = total + stencils[first + 1] * shifted(values, 1, 0)
        total = total + stencils[first + 2] * shifted(values, -1, 1)
        return total + stencils[first + 3] * shifted(values, 1, 1)

    own_grad.wait()
    for offset in range(1, mem_count):
        across(jnp.int32(offset)).wait_recv()
    for_targets(lambda number, direction: grad_copy(number, direction).start())
    for_sources(lambda number, direction: pert_copy(number, direction).wait_recv())

    def build(group, carry):
        south = folded(recv_rows[0, group].astype(jnp.float32), cols)
        north = folded(recv_rows[1, group].astype(jnp.float32), cols)
        from_east = recv_cols[0, group].astype(jnp.float32)
        from_west = recv_cols[1, group].astype(jnp.float32)
        blocks = []
        for k in range(per_mem):
            block = centre[k, peer(group)].astype(jnp.float32)
            tile = slice((k // 2) * SUB, (k // 2 + 1) * SUB)
            south_rows, north_rows = south[tile], north[tile]
            if k % 2:
                south_rows = pltpu.roll(south_rows, HALO, 0)
                north_rows = pltpu.roll(north_rows, HALO, 0)
            east = pltpu.roll(from_east, LANES - HALO * k, 1) if k else from_east
            west = pltpu.roll(from_west, (-HALO * (k + 1)) % LANES, 1)
            side = jnp.where(lane < LANES // 2, east, west)
            block = circular(
                jnp.concatenate([block, side], axis=1), north_rows, south_rows, low_row_full
            )
            blocks.append(jnp.where(scaled[1] > 0.5, block, 0.0))
        missing = perm_rows.shape[1] - per_mem * full_rows
        if missing:
            blocks.append(jnp.zeros((missing, full_cols), jnp.float32))
        stack = jnp.concatenate(blocks, axis=0).astype(jnp.bfloat16)
        stack = product(stack, perm_cols[...]).astype(jnp.bfloat16)
        field[group] = product(perm_rows[...], stack)
        return carry

    lax.fori_loop(0, mem_count, build, 0)
    for_sources(lambda number, direction: grad_copy(number, direction).wait_recv())

    def step_work(step, carry):
        group = group_at(step)
        scaled[0] = extended(grads[group])
        total = jnp.zeros((full_rows, full_cols), jnp.float32)
        for k in range(per_mem):
            here = slice(k * full_rows, (k + 1) * full_rows)
            values = field[group, here] * scaled[0]
            values = one_pass(values, 5)
            values = one_pass(values, 5)
            values = one_pass(values, 1)
            values = one_pass(values, 1)
            total = total + values * field[group, here]
        total = product(parts_of(total), back_cols[...]).astype(jnp.bfloat16)
        sums[0, group] = product(back_parts[...], total)

        @pl.when(step + 1 < mem_count)
        def _():
            back(group).start()

        return carry

    lax.fori_loop(0, mem_count, step_work, 0)
    total = sums[0, 0]
    for offset in range(1, mem_count):
        back(jnp.int32(offset)).wait_recv()
        total = total + sums[1, offset]
    out[0] = total * scale

    for offset in range(1, mem_count):
        across(jnp.int32(offset)).wait_send()
        back(jnp.int32(offset)).wait_send()

    def sent(number, direction):
        for copy in (coef_copy, grad_copy, pert_copy):
            copy(number, direction).wait_send()

    for_targets(sent)


def body(mesh_sizes, gradient, perturbations, filter_coef):
    mem_count, lat_count, lon_count = mesh_sizes
    levels, rows, cols = gradient.shape
    per_mem = perturbations.shape[0]
    members = per_mem * mem_count
    assert mem_count & (mem_count - 1) == 0 and HALO * per_mem <= LANES
    assert levels == 1 and rows % 16 == 0 and cols % LANES == 0
    full_rows, full_cols = rows + 2 * HALO, cols + LANES
    packed = (per_mem + 3) // 4 * 2 * SUB
    sizes = (mem_count, lat_count, lon_count, 1.0 / (members - 1))
    return pl.pallas_call(
        functools.partial(kernel, sizes),
        out_shape=jax.ShapeDtypeStruct(gradient.shape, jnp.float32),
        in_specs=[pl.BlockSpec(memory_space=pltpu.HBM)] * 3,
        out_specs=pl.BlockSpec(memory_space=pltpu.VMEM),
        scratch_shapes=[
            pltpu.VMEM((per_mem, mem_count, rows, cols), jnp.bfloat16),
            pltpu.VMEM((mem_count, per_mem * full_rows, full_cols), jnp.float32),
            pltpu.VMEM((2, mem_count, packed, cols), jnp.bfloat16),
            pltpu.VMEM((2, mem_count, rows, LANES), jnp.bfloat16),
            pltpu.VMEM((2, mem_count, packed, cols + 2 * LANES), jnp.bfloat16),
            pltpu.VMEM((2, mem_count, rows, LANES), jnp.bfloat16),
            pltpu.VMEM((5, rows + 2 * SUB, cols + 2 * LANES), jnp.float32),
            pltpu.VMEM((9, full_rows, full_cols), jnp.float32),
            pltpu.VMEM((2, full_rows, full_cols), jnp.float32),
            pltpu.VMEM((mem_count, rows + 2 * SUB, cols + 2 * LANES), jnp.float32),
            pltpu.VMEM((2, mem_count, rows, cols), jnp.float32),
            pltpu.VMEM((full_cols, full_cols), jnp.bfloat16),
            pltpu.VMEM((per_mem * full_rows, -(-per_mem * full_rows // 16) * 16), jnp.bfloat16),
            pltpu.VMEM((full_rows, 3 * full_rows + SUB), jnp.bfloat16),
            pltpu.VMEM((full_cols, cols), jnp.bfloat16),
            pltpu.VMEM((rows, 3 * full_rows + SUB), jnp.bfloat16),
            pltpu.SemaphoreType.DMA((mem_count,)),
            pltpu.SemaphoreType.DMA((mem_count,)),
            pltpu.SemaphoreType.DMA((mem_count,)),
            pltpu.SemaphoreType.DMA((mem_count,)),
            pltpu.SemaphoreType.DMA((3, len(DIRECTIONS))),
            pltpu.SemaphoreType.DMA((3, len(DIRECTIONS))),
            pltpu.SemaphoreType.DMA((3,)),
        ],
        compiler_params=pltpu.CompilerParams(
            collective_id=0, has_side_effects=True, vmem_limit_bytes=60 * 1024 * 1024
        ),
    )(perturbations, gradient, filter_coef)


def solution(mesh):
    sizes = tuple(mesh.shape[name] for name in ("mem", "lat", "lon"))
    return jax.shard_map(
        functools.partial(body, sizes),
        mesh=mesh,
        in_specs=(P("mem", "lat", "lon"), P("mem", None, "lat", "lon"), P(None, "lat", "lon")),
        out_specs=P("mem", "lat", "lon"),
        check_vma=False,
    )
```

```python
import functools

import jax
import jax.numpy as jnp
from jax import lax
from jax.experimental import pallas as pl
from jax.experimental.pallas import tpu as pltpu
from jax.sharding import PartitionSpec as P

HALO = 4
LANES = 128
SUB = 8
DIRECTIONS = ((-1, 0), (1, 0), (0, -1), (0, 1), (-1, -1), (-1, 1), (1, -1), (1, 1))


def shifted(values, offset, axis):
    size = values.shape[axis]
    if axis == 1:
        return pltpu.roll(values, (-offset) % size, 1)
    if offset < 0:
        edge = pltpu.roll(values[size - SUB :], 1, 0)
        return jnp.concatenate([edge, values[: size - SUB]], axis=0)
    edge = pltpu.roll(values[:SUB], SUB - 1, 0)
    return jnp.concatenate([values[SUB:], edge], axis=0)


def place_of(index, unit, size):
    return (index % unit) * (size // unit) + index // unit


def columns_of(values):
    return [values[:, low : low + LANES] for low in range(0, values.shape[1], LANES)]


def interleaved(ref, values):
    tiles = values.shape[0] // SUB
    for u, column in enumerate(columns_of(values)):
        ref[u] = column
    return jnp.concatenate(
        [
            jnp.concatenate(
                [ref[u, pl.ds(t, SUB, stride=tiles), :] for t in range(tiles)], axis=0
            )
            for u in range(ref.shape[0])
        ],
        axis=1,
    )


def circular(centre_rows, north_rows, south_rows, row_low):
    return jnp.concatenate([centre_rows, jnp.where(row_low, south_rows, north_rows)], axis=0)


def folded(padded, cols):
    low = lax.broadcasted_iota(jnp.int32, (padded.shape[0], LANES), 1) < LANES // 2
    side = jnp.where(low, padded[:, LANES + cols :], padded[:, :LANES])
    return jnp.concatenate([padded[:, LANES : LANES + cols], side], axis=1)


def kernel(
    sizes,
    pert,
    grad,
    coef,
    out,
    centre,
    field,
    send_rows,
    send_cols,
    recv_rows,
    recv_cols,
    ext,
    stencils,
    scaled,
    grads,
    sums,
    wide_sums,
    natural,
    z_send,
    z_recv,
    sum_send,
    sum_recv,
    halo_send,
    halo_recv,
    local_sem,
):
    mem_count, lat_count, lon_count, scale = sizes
    per_mem, _, rows, cols = pert.shape
    mem, lat, lon = (lax.axis_index(name) for name in ("mem", "lat", "lon"))
    mesh_id = pl.DeviceIdType.MESH

    def present(direction):
        up, right = direction
        checks = []
        if up:
            checks.append(lat > 0 if up < 0 else lat < lat_count - 1)
        if right:
            checks.append(lon > 0 if right < 0 else lon < lon_count - 1)
        return functools.reduce(jnp.logical_and, checks)

    def neighbour(direction):
        return (mem, lat + direction[0], lon + direction[1])

    def peer(offset):
        total, bit = 0, 1
        while bit < mem_count:
            total = total + bit * lax.rem(lax.div(mem, bit) + lax.div(offset, bit), 2)
            bit *= 2
        return total

    def group_at(step):
        return lax.rem(step + 1, mem_count)

    barrier = pltpu.get_barrier_semaphore()
    for offset in range(1, mem_count):
        pl.semaphore_signal(barrier, inc=1, device_id=(peer(jnp.int32(offset)), lat, lon), device_id_type=mesh_id)
    for direction in DIRECTIONS:

        @pl.when(present(direction))
        def _():
            pl.semaphore_signal(barrier, inc=1, device_id=neighbour(direction), device_id_type=mesh_id)

    inner_rows, inner_cols = pl.ds(SUB, rows), pl.ds(LANES, cols)

    own_pert = pltpu.make_async_copy(pert, centre, local_sem.at[2])
    own_grad = pltpu.make_async_copy(
        grad.at[0], grads.at[0, inner_rows, inner_cols], local_sem.at[0]
    )
    own_coef = pltpu.make_async_copy(
        coef, ext.at[:, inner_rows, inner_cols], local_sem.at[1]
    )
    own_pert.start()
    own_grad.start()
    own_coef.start()

    full_rows, full_cols = rows + 2 * HALO, cols + LANES

    def inside_of(row_index, col_index):
        row_index = jnp.where(row_index < rows + HALO, row_index, row_index - full_rows)
        col_index = jnp.where(col_index < cols + LANES // 2, col_index, col_index - full_cols)
        near = (col_index >= -HALO) & (col_index < cols + HALO)
        row_index = row_index + lat * rows
        col_index = col_index + lon * cols
        return (
            near
            & (row_index >= 0)
            & (row_index < rows * lat_count)
            & (col_index >= 0)
            & (col_index < cols * lon_count)
        )

    row_index, col_index = (
        lax.broadcasted_iota(jnp.int32, (full_rows, full_cols), axis) for axis in range(2)
    )
    inside = inside_of(row_index, col_index)
    scaled[1] = inside.astype(jnp.float32)
    inside_here = inside_of(place_of(row_index, SUB, full_rows), col_index)
    low_row_full = lax.broadcasted_iota(jnp.int32, (SUB, full_cols), 0) < HALO

    blocks = [
        1 + jnp.where(here > 0, 1, 0) + jnp.where(here < count - 1, 1, 0)
        for here, count in ((lat, lat_count), (lon, lon_count))
    ]
    pl.semaphore_wait(barrier, mem_count - 2 + blocks[0] * blocks[1])

    def across(offset):
        return pltpu.make_async_remote_copy(
            src_ref=grad.at[0],
            dst_ref=grads.at[offset, inner_rows, inner_cols],
            send_sem=z_send.at[offset],
            recv_sem=z_recv.at[offset],
            device_id=(peer(offset), lat, lon),
            device_id_type=mesh_id,
        )

    def back(offset):
        return pltpu.make_async_remote_copy(
            src_ref=wide_sums.at[offset, :, pl.ds(0, rows)],
            dst_ref=sums.at[offset],
            send_sem=sum_send.at[offset],
            recv_sem=sum_recv.at[offset],
            device_id=(peer(offset), lat, lon),
            device_id_type=mesh_id,
        )

    for offset in range(1, mem_count):
        across(jnp.int32(offset)).start()

    def span(step, low, size, edge):
        if step == 0:
            return pl.ds(0, size), pl.ds(low, size)
        if step < 0:
            return pl.ds(0, edge), pl.ds(low + size, edge)
        return pl.ds(size - edge, edge), pl.ds(low - edge, edge)

    def coef_copy(number, direction):
        source_rows, target_rows = span(direction[0], SUB, rows, SUB)
        source_cols, target_cols = span(direction[1], LANES, cols, LANES)
        return pltpu.make_async_remote_copy(
            src_ref=coef.at[:, source_rows, source_cols],
            dst_ref=ext.at[:, target_rows, target_cols],
            send_sem=halo_send.at[0, number],
            recv_sem=halo_recv.at[0, number],
            device_id=neighbour(direction),
            device_id_type=mesh_id,
        )

    def grad_copy(number, direction):
        source_rows, target_rows = span(direction[0], SUB, rows, SUB)
        source_cols, target_cols = span(direction[1], LANES, cols, LANES)
        source_rows = pl.ds(source_rows.start + SUB, source_rows.size)
        source_cols = pl.ds(source_cols.start + LANES, source_cols.size)
        return pltpu.make_async_remote_copy(
            src_ref=grads.at[:, source_rows, source_cols],
            dst_ref=grads.at[:, target_rows, target_cols],
            send_sem=halo_send.at[1, number],
            recv_sem=halo_recv.at[1, number],
            device_id=neighbour(direction),
            device_id_type=mesh_id,
        )

    def pert_copy(number, direction):
        up, right = direction
        if up == 0:
            side = 0 if right < 0 else 1
            source, target = send_cols.at[side], recv_cols.at[side]
        else:
            side = 0 if up < 0 else 1
            source_cols, target_cols = span(right, LANES, cols, LANES)
            source = send_rows.at[side, :, :, source_cols]
            target = recv_rows.at[side, :, :, target_cols]
        return pltpu.make_async_remote_copy(
            src_ref=source,
            dst_ref=target,
            send_sem=halo_send.at[2, number],
            recv_sem=halo_recv.at[2, number],
            device_id=neighbour(direction),
            device_id_type=mesh_id,
        )

    def for_targets(action):
        for number, direction in enumerate(DIRECTIONS):

            @pl.when(present(direction))
            def _():
                action(number, direction)

    def for_sources(action):
        for number, direction in enumerate(DIRECTIONS):

            @pl.when(present((-direction[0], -direction[1])))
            def _():
                action(number, direction)

    for_targets(lambda number, direction: coef_copy(number, direction).start())

    low_row = lax.broadcasted_iota(jnp.int32, (SUB, cols), 0) < HALO
    lane = lax.broadcasted_iota(jnp.int32, (rows, LANES), 1)
    tiles = send_rows.shape[2] // SUB

    def pack(group, carry):
        tops, bottoms = [], []
        west = east = None
        for k in range(per_mem):
            block = centre[k, peer(group)].astype(jnp.float32)
            top, bottom = block[:SUB], block[rows - SUB :]
            if k % 2:
                tops[-1] = jnp.where(low_row, tops[-1], pltpu.roll(top, HALO, 0))
                bottoms[-1] = jnp.where(low_row, pltpu.roll(bottom, HALO, 0), bottoms[-1])
            else:
                tops.append(top)
                bottoms.append(bottom)
            place = (lane >= HALO * k) & (lane < HALO * (k + 1))
            first = pltpu.roll(block[:, :LANES], HALO * k, 1) if k else block[:, :LANES]
            last = pltpu.roll(block[:, cols - LANES :], HALO * (k + 1) % LANES, 1)
            west = first if west is None else jnp.where(place, first, west)
            east = last if east is None else jnp.where(place, last, east)
        while len(tops) < tiles:
            tops.append(tops[-1])
            bottoms.append(bottoms[-1])
        send_rows[0, group] = jnp.concatenate(tops, axis=0).astype(jnp.bfloat16)
        send_rows[1, group] = jnp.concatenate(bottoms, axis=0).astype(jnp.bfloat16)
        send_cols[0, group] = west.astype(jnp.bfloat16)
        send_cols[1, group] = east.astype(jnp.bfloat16)
        return carry

    own_pert.wait()
    lax.fori_loop(0, mem_count, pack, 0)
    for_targets(lambda number, direction: pert_copy(number, direction).start())
    own_coef.wait()
    for_sources(lambda number, direction: coef_copy(number, direction).wait_recv())

    def extended(block, slot):
        wide = folded(block, cols)
        wide = circular(
            wide[SUB : SUB + rows], wide[:SUB], wide[SUB + rows :], low_row_full
        )
        return interleaved(natural.at[slot], jnp.where(scaled[1] > 0.5, wide, 0.0))

    c0, cn, cs, cw, ce = (extended(ext[index], index) for index in range(5))
    for index, value in enumerate((c0, cn, cs, cw, ce)):
        stencils[index] = value
    for index, value in enumerate(
        (shifted(cs, -1, 0), shifted(cn, 1, 0), shifted(ce, -1, 1), shifted(cw, 1, 1))
    ):
        stencils[5 + index] = jnp.where(inside_here, value, 0.0)

    def one_pass(values, first):
        total = stencils[0] * values + stencils[first] * shifted(values, -1, 0)
        total = total + stencils[first + 1] * shifted(values, 1, 0)
        total = total + stencils[first + 2] * shifted(values, -1, 1)
        return total + stencils[first + 3] * shifted(values, 1, 1)

    own_grad.wait()
    for offset in range(1, mem_count):
        across(jnp.int32(offset)).wait_recv()
    for_targets(lambda number, direction: grad_copy(number, direction).start())
    for_sources(lambda number, direction: pert_copy(number, direction).wait_recv())

    def build(group, carry):
        south = folded(recv_rows[0, group].astype(jnp.float32), cols)
        north = folded(recv_rows[1, group].astype(jnp.float32), cols)
        from_east = recv_cols[0, group].astype(jnp.float32)
        from_west = recv_cols[1, group].astype(jnp.float32)
        for k in range(per_mem):
            block = centre[k, peer(group)].astype(jnp.float32)
            tile = slice((k // 2) * SUB, (k // 2 + 1) * SUB)
            south_rows, north_rows = south[tile], north[tile]
            if k % 2:
                south_rows = pltpu.roll(south_rows, HALO, 0)
                north_rows = pltpu.roll(north_rows, HALO, 0)
            east = pltpu.roll(from_east, LANES - HALO * k, 1) if k else from_east
            west = pltpu.roll(from_west, (-HALO * (k + 1)) % LANES, 1)
            side = jnp.where(lane < LANES // 2, east, west)
            block = circular(
                jnp.concatenate([block, side], axis=1), north_rows, south_rows, low_row_full
            )
            block = jnp.where(scaled[1] > 0.5, block, 0.0)
            field[group, k] = interleaved(natural.at[k], block)
        return carry

    lax.fori_loop(0, mem_count, build, 0)
    for_sources(lambda number, direction: grad_copy(number, direction).wait_recv())

    def step_work(step, carry):
        group = group_at(step)
        scaled[0] = extended(grads[group], 0)
        total = jnp.zeros((full_rows, cols), jnp.float32)
        for k in range(per_mem):
            values = field[group, k] * scaled[0]
            values = one_pass(values, 5)
            values = one_pass(values, 5)
            values = one_pass(values, 1)
            values = one_pass(values, 1)
            total = total + values[:, :cols] * field[group, k, :, :cols]
        tiles = full_rows // SUB
        for u, column in enumerate(columns_of(total)):
            for t in range(tiles):
                wide_sums[group, u, pl.ds(t, SUB, stride=tiles), :] = column[
                    t * SUB : (t + 1) * SUB
                ]

        @pl.when(step + 1 < mem_count)
        def _():
            back(group).start()

        return carry

    lax.fori_loop(0, mem_count, step_work, 0)
    total = wide_sums[0, :, :rows]
    for offset in range(1, mem_count):
        back(jnp.int32(offset)).wait_recv()
        total = total + sums[offset]
    for u in range(cols // LANES):
        out[0, :, u * LANES : (u + 1) * LANES] = total[u] * scale

    for offset in range(1, mem_count):
        across(jnp.int32(offset)).wait_send()
        back(jnp.int32(offset)).wait_send()

    def sent(number, direction):
        for copy in (coef_copy, grad_copy, pert_copy):
            copy(number, direction).wait_send()

    for_targets(sent)


def body(mesh_sizes, gradient, perturbations, filter_coef):
    mem_count, lat_count, lon_count = mesh_sizes
    levels, rows, cols = gradient.shape
    per_mem = perturbations.shape[0]
    members = per_mem * mem_count
    assert mem_count & (mem_count - 1) == 0 and HALO * per_mem <= LANES
    assert levels == 1 and rows % 16 == 0 and cols % LANES == 0
    full_rows, full_cols = rows + 2 * HALO, cols + LANES
    packed = (per_mem + 3) // 4 * 2 * SUB
    sizes = (mem_count, lat_count, lon_count, 1.0 / (members - 1))
    return pl.pallas_call(
        functools.partial(kernel, sizes),
        out_shape=jax.ShapeDtypeStruct(gradient.shape, jnp.float32),
        in_specs=[pl.BlockSpec(memory_space=pltpu.HBM)] * 3,
        out_specs=pl.BlockSpec(memory_space=pltpu.VMEM),
        scratch_shapes=[
            pltpu.VMEM((per_mem, mem_count, rows, cols), jnp.bfloat16),
            pltpu.VMEM((mem_count, per_mem, full_rows, full_cols), jnp.float32),
            pltpu.VMEM((2, mem_count, packed, cols), jnp.bfloat16),
            pltpu.VMEM((2, mem_count, rows, LANES), jnp.bfloat16),
            pltpu.VMEM((2, mem_count, packed, cols + 2 * LANES), jnp.bfloat16),
            pltpu.VMEM((2, mem_count, rows, LANES), jnp.bfloat16),
            pltpu.VMEM((5, rows + 2 * SUB, cols + 2 * LANES), jnp.float32),
            pltpu.VMEM((9, full_rows, full_cols), jnp.float32),
            pltpu.VMEM((2, full_rows, full_cols), jnp.float32),
            pltpu.VMEM((mem_count, rows + 2 * SUB, cols + 2 * LANES), jnp.float32),
            pltpu.VMEM((mem_count, cols // LANES, rows, LANES), jnp.float32),
            pltpu.VMEM((mem_count, cols // LANES, full_rows, LANES), jnp.float32),
            pltpu.VMEM((max(5, per_mem), full_cols // LANES, full_rows, LANES), jnp.float32),
            pltpu.SemaphoreType.DMA((mem_count,)),
            pltpu.SemaphoreType.DMA((mem_count,)),
            pltpu.SemaphoreType.DMA((mem_count,)),
            pltpu.SemaphoreType.DMA((mem_count,)),
            pltpu.SemaphoreType.DMA((3, len(DIRECTIONS))),
            pltpu.SemaphoreType.DMA((3, len(DIRECTIONS))),
            pltpu.SemaphoreType.DMA((3,)),
        ],
        compiler_params=pltpu.CompilerParams(
            collective_id=0, has_side_effects=True, vmem_limit_bytes=60 * 1024 * 1024
        ),
    )(perturbations, gradient, filter_coef)


def solution(mesh):
    sizes = tuple(mesh.shape[name] for name in ("mem", "lat", "lon"))
    return jax.shard_map(
        functools.partial(body, sizes),
        mesh=mesh,
        in_specs=(P("mem", "lat", "lon"), P("mem", None, "lat", "lon"), P(None, "lat", "lon")),
        out_specs=P("mem", "lat", "lon"),
        check_vma=False,
    )
```

```python
import functools

import jax
import jax.numpy as jnp
from jax import lax
from jax.experimental import pallas as pl
from jax.experimental.pallas import tpu as pltpu
from jax.sharding import PartitionSpec as P

HALO = 4
LANES = 128
SUB = 8
DIRECTIONS = ((-1, 0), (1, 0), (0, -1), (0, 1), (-1, -1), (-1, 1), (1, -1), (1, 1))


def shifted(values, offset, axis):
    size = values.shape[axis]
    if axis == 1:
        return pltpu.roll(values, (-offset) % size, 1)
    if offset < 0:
        edge = pltpu.roll(values[size - SUB :], 1, 0)
        return jnp.concatenate([edge, values[: size - SUB]], axis=0)
    edge = pltpu.roll(values[:SUB], SUB - 1, 0)
    return jnp.concatenate([values[SUB:], edge], axis=0)


def place_of(index, unit, size):
    return (index % unit) * (size // unit) + index // unit


def columns_of(values):
    return [values[:, low : low + LANES] for low in range(0, values.shape[1], LANES)]


def interleaved(ref, values):
    tiles = values.shape[0] // SUB
    for u, column in enumerate(columns_of(values)):
        ref[u] = column
    return jnp.concatenate(
        [
            jnp.concatenate(
                [ref[u, pl.ds(t, SUB, stride=tiles), :] for t in range(tiles)], axis=0
            )
            for u in range(ref.shape[0])
        ],
        axis=1,
    )


def circular(centre_rows, north_rows, south_rows, row_low):
    return jnp.concatenate([centre_rows, jnp.where(row_low, south_rows, north_rows)], axis=0)


def folded(padded, cols):
    low = lax.broadcasted_iota(jnp.int32, (padded.shape[0], LANES), 1) < LANES // 2
    side = jnp.where(low, padded[:, LANES + cols :], padded[:, :LANES])
    return jnp.concatenate([padded[:, LANES : LANES + cols], side], axis=1)


def kernel(
    sizes,
    pert,
    grad,
    coef,
    out,
    centre,
    field,
    send_rows,
    send_cols,
    recv_rows,
    recv_cols,
    ext,
    stencils,
    scaled,
    grads,
    sums,
    wide_sums,
    natural,
    z_send,
    z_recv,
    sum_send,
    sum_recv,
    halo_send,
    halo_recv,
    local_sem,
):
    mem_count, lat_count, lon_count, scale = sizes
    per_mem, _, rows, cols = pert.shape
    mem, lat, lon = (lax.axis_index(name) for name in ("mem", "lat", "lon"))
    mesh_id = pl.DeviceIdType.MESH

    def present(direction):
        up, right = direction
        checks = []
        if up:
            checks.append(lat > 0 if up < 0 else lat < lat_count - 1)
        if right:
            checks.append(lon > 0 if right < 0 else lon < lon_count - 1)
        return functools.reduce(jnp.logical_and, checks)

    def neighbour(direction):
        return (mem, lat + direction[0], lon + direction[1])

    def peer(offset):
        total, bit = 0, 1
        while bit < mem_count:
            total = total + bit * lax.rem(lax.div(mem, bit) + lax.div(offset, bit), 2)
            bit *= 2
        return total

    def group_at(step):
        return lax.rem(step + 1, mem_count)

    barrier = pltpu.get_barrier_semaphore()
    for offset in range(1, mem_count):
        pl.semaphore_signal(barrier, inc=1, device_id=(peer(jnp.int32(offset)), lat, lon), device_id_type=mesh_id)
    for direction in DIRECTIONS:

        @pl.when(present(direction))
        def _():
            pl.semaphore_signal(barrier, inc=1, device_id=neighbour(direction), device_id_type=mesh_id)

    inner_rows, inner_cols = pl.ds(SUB, rows), pl.ds(LANES, cols)

    own_pert = pltpu.make_async_copy(pert, centre, local_sem.at[2])
    own_grad = pltpu.make_async_copy(
        grad.at[0], grads.at[0, inner_rows, inner_cols], local_sem.at[0]
    )
    own_coef = pltpu.make_async_copy(
        coef, ext.at[:, inner_rows, inner_cols], local_sem.at[1]
    )
    own_pert.start()
    own_grad.start()
    own_coef.start()

    full_rows, full_cols = rows + 2 * HALO, cols + LANES

    def inside_of(row_index, col_index):
        row_index = jnp.where(row_index < rows + HALO, row_index, row_index - full_rows)
        col_index = jnp.where(col_index < cols + LANES // 2, col_index, col_index - full_cols)
        near = (col_index >= -HALO) & (col_index < cols + HALO)
        row_index = row_index + lat * rows
        col_index = col_index + lon * cols
        return (
            near
            & (row_index >= 0)
            & (row_index < rows * lat_count)
            & (col_index >= 0)
            & (col_index < cols * lon_count)
        )

    row_index, col_index = (
        lax.broadcasted_iota(jnp.int32, (full_rows, full_cols), axis) for axis in range(2)
    )
    inside = inside_of(row_index, col_index)
    scaled[1] = inside.astype(jnp.float32)
    inside_here = inside_of(place_of(row_index, SUB, full_rows), col_index)
    low_row_full = lax.broadcasted_iota(jnp.int32, (SUB, full_cols), 0) < HALO

    blocks = [
        1 + jnp.where(here > 0, 1, 0) + jnp.where(here < count - 1, 1, 0)
        for here, count in ((lat, lat_count), (lon, lon_count))
    ]
    pl.semaphore_wait(barrier, mem_count - 2 + blocks[0] * blocks[1])

    def across(offset):
        return pltpu.make_async_remote_copy(
            src_ref=grad.at[0],
            dst_ref=grads.at[offset, inner_rows, inner_cols],
            send_sem=z_send.at[offset],
            recv_sem=z_recv.at[offset],
            device_id=(peer(offset), lat, lon),
            device_id_type=mesh_id,
        )

    def back(offset):
        return pltpu.make_async_remote_copy(
            src_ref=wide_sums.at[offset, :, pl.ds(0, rows)],
            dst_ref=sums.at[offset],
            send_sem=sum_send.at[offset],
            recv_sem=sum_recv.at[offset],
            device_id=(peer(offset), lat, lon),
            device_id_type=mesh_id,
        )

    for offset in range(1, mem_count):
        across(jnp.int32(offset)).start()

    def span(step, low, size, edge):
        if step == 0:
            return pl.ds(0, size), pl.ds(low, size)
        if step < 0:
            return pl.ds(0, edge), pl.ds(low + size, edge)
        return pl.ds(size - edge, edge), pl.ds(low - edge, edge)

    def coef_copy(number, direction):
        source_rows, target_rows = span(direction[0], SUB, rows, SUB)
        source_cols, target_cols = span(direction[1], LANES, cols, LANES)
        return pltpu.make_async_remote_copy(
            src_ref=coef.at[:, source_rows, source_cols],
            dst_ref=ext.at[:, target_rows, target_cols],
            send_sem=halo_send.at[0, number],
            recv_sem=halo_recv.at[0, number],
            device_id=neighbour(direction),
            device_id_type=mesh_id,
        )

    def grad_copy(number, direction):
        source_rows, target_rows = span(direction[0], SUB, rows, SUB)
        source_cols, target_cols = span(direction[1], LANES, cols, LANES)
        source_rows = pl.ds(source_rows.start + SUB, source_rows.size)
        source_cols = pl.ds(source_cols.start + LANES, source_cols.size)
        return pltpu.make_async_remote_copy(
            src_ref=grads.at[:, source_rows, source_cols],
            dst_ref=grads.at[:, target_rows, target_cols],
            send_sem=halo_send.at[1, number],
            recv_sem=halo_recv.at[1, number],
            device_id=neighbour(direction),
            device_id_type=mesh_id,
        )

    def pert_copy(number, direction):
        up, right = direction
        if up == 0:
            side = 0 if right < 0 else 1
            source, target = send_cols.at[side], recv_cols.at[side]
        else:
            side = 0 if up < 0 else 1
            source_cols, target_cols = span(right, LANES, cols, LANES)
            source = send_rows.at[side, :, :, source_cols]
            target = recv_rows.at[side, :, :, target_cols]
        return pltpu.make_async_remote_copy(
            src_ref=source,
            dst_ref=target,
            send_sem=halo_send.at[2, number],
            recv_sem=halo_recv.at[2, number],
            device_id=neighbour(direction),
            device_id_type=mesh_id,
        )

    def for_targets(action):
        for number, direction in enumerate(DIRECTIONS):

            @pl.when(present(direction))
            def _():
                action(number, direction)

    def for_sources(action):
        for number, direction in enumerate(DIRECTIONS):

            @pl.when(present((-direction[0], -direction[1])))
            def _():
                action(number, direction)

    for_targets(lambda number, direction: coef_copy(number, direction).start())

    low_row = lax.broadcasted_iota(jnp.int32, (SUB, cols), 0) < HALO
    lane = lax.broadcasted_iota(jnp.int32, (rows, LANES), 1)
    tiles = send_rows.shape[2] // SUB

    def pack(group, carry):
        tops, bottoms = [], []
        west = east = None
        for k in range(per_mem):
            block = centre[k, peer(group)].astype(jnp.float32)
            top, bottom = block[:SUB], block[rows - SUB :]
            if k % 2:
                tops[-1] = jnp.where(low_row, tops[-1], pltpu.roll(top, HALO, 0))
                bottoms[-1] = jnp.where(low_row, pltpu.roll(bottom, HALO, 0), bottoms[-1])
            else:
                tops.append(top)
                bottoms.append(bottom)
            place = (lane >= HALO * k) & (lane < HALO * (k + 1))
            first = pltpu.roll(block[:, :LANES], HALO * k, 1) if k else block[:, :LANES]
            last = pltpu.roll(block[:, cols - LANES :], HALO * (k + 1) % LANES, 1)
            west = first if west is None else jnp.where(place, first, west)
            east = last if east is None else jnp.where(place, last, east)
        while len(tops) < tiles:
            tops.append(tops[-1])
            bottoms.append(bottoms[-1])
        send_rows[0, group] = jnp.concatenate(tops, axis=0).astype(jnp.bfloat16)
        send_rows[1, group] = jnp.concatenate(bottoms, axis=0).astype(jnp.bfloat16)
        send_cols[0, group] = west.astype(jnp.bfloat16)
        send_cols[1, group] = east.astype(jnp.bfloat16)
        return carry

    own_pert.wait()
    lax.fori_loop(0, mem_count, pack, 0)
    for_targets(lambda number, direction: pert_copy(number, direction).start())
    own_coef.wait()
    for_sources(lambda number, direction: coef_copy(number, direction).wait_recv())

    def extended(block, slot):
        wide = folded(block, cols)
        wide = circular(
            wide[SUB : SUB + rows], wide[:SUB], wide[SUB + rows :], low_row_full
        )
        return interleaved(natural.at[slot], jnp.where(scaled[1] > 0.5, wide, 0.0))

    c0, cn, cs, cw, ce = (extended(ext[index], index) for index in range(5))
    for index, value in enumerate((c0, cn, cs, cw, ce)):
        stencils[index] = value
    for index, value in enumerate(
        (shifted(cs, -1, 0), shifted(cn, 1, 0), shifted(ce, -1, 1), shifted(cw, 1, 1))
    ):
        stencils[5 + index] = jnp.where(inside_here, value, 0.0)

    def one_pass(values, first):
        total = stencils[0] * values + stencils[first] * shifted(values, -1, 0)
        total = total + stencils[first + 1] * shifted(values, 1, 0)
        total = total + stencils[first + 2] * shifted(values, -1, 1)
        return total + stencils[first + 3] * shifted(values, 1, 1)

    own_grad.wait()
    for offset in range(1, mem_count):
        across(jnp.int32(offset)).wait_recv()
    for_targets(lambda number, direction: grad_copy(number, direction).start())
    for_sources(lambda number, direction: pert_copy(number, direction).wait_recv())

    def build(group, carry):
        south = folded(recv_rows[0, group].astype(jnp.float32), cols)
        north = folded(recv_rows[1, group].astype(jnp.float32), cols)
        from_east = recv_cols[0, group].astype(jnp.float32)
        from_west = recv_cols[1, group].astype(jnp.float32)
        for k in range(per_mem):
            block = centre[k, peer(group)].astype(jnp.float32)
            tile = slice((k // 2) * SUB, (k // 2 + 1) * SUB)
            south_rows, north_rows = south[tile], north[tile]
            if k % 2:
                south_rows = pltpu.roll(south_rows, HALO, 0)
                north_rows = pltpu.roll(north_rows, HALO, 0)
            east = pltpu.roll(from_east, LANES - HALO * k, 1) if k else from_east
            west = pltpu.roll(from_west, (-HALO * (k + 1)) % LANES, 1)
            side = jnp.where(lane < LANES // 2, east, west)
            block = circular(
                jnp.concatenate([block, side], axis=1), north_rows, south_rows, low_row_full
            )
            block = jnp.where(scaled[1] > 0.5, block, 0.0)
            field[group, k] = interleaved(natural.at[k], block)
        return carry

    lax.fori_loop(0, mem_count, build, 0)
    for_sources(lambda number, direction: grad_copy(number, direction).wait_recv())

    def step_work(step, carry):
        group = group_at(step)
        scaled[0] = extended(grads[group], 0)
        total = jnp.zeros((full_rows, cols), jnp.float32)

        def member(k, total):
            values = field[group, k] * scaled[0]
            values = one_pass(values, 5)
            values = one_pass(values, 5)
            values = one_pass(values, 1)
            values = one_pass(values, 1)
            return total + values[:, :cols] * field[group, k, :, :cols]

        total = lax.fori_loop(0, per_mem, member, total)
        tiles = full_rows // SUB
        for u, column in enumerate(columns_of(total)):
            for t in range(tiles):
                wide_sums[group, u, pl.ds(t, SUB, stride=tiles), :] = column[
                    t * SUB : (t + 1) * SUB
                ]

        @pl.when(step + 1 < mem_count)
        def _():
            back(group).start()

        return carry

    lax.fori_loop(0, mem_count, step_work, 0)
    total = wide_sums[0, :, :rows]
    for offset in range(1, mem_count):
        back(jnp.int32(offset)).wait_recv()
        total = total + sums[offset]
    for u in range(cols // LANES):
        out[0, :, u * LANES : (u + 1) * LANES] = total[u] * scale

    for offset in range(1, mem_count):
        across(jnp.int32(offset)).wait_send()
        back(jnp.int32(offset)).wait_send()

    def sent(number, direction):
        for copy in (coef_copy, grad_copy, pert_copy):
            copy(number, direction).wait_send()

    for_targets(sent)


def body(mesh_sizes, gradient, perturbations, filter_coef):
    mem_count, lat_count, lon_count = mesh_sizes
    levels, rows, cols = gradient.shape
    per_mem = perturbations.shape[0]
    members = per_mem * mem_count
    assert mem_count & (mem_count - 1) == 0 and HALO * per_mem <= LANES
    assert levels == 1 and rows % 16 == 0 and cols % LANES == 0
    full_rows, full_cols = rows + 2 * HALO, cols + LANES
    packed = (per_mem + 3) // 4 * 2 * SUB
    sizes = (mem_count, lat_count, lon_count, 1.0 / (members - 1))
    return pl.pallas_call(
        functools.partial(kernel, sizes),
        out_shape=jax.ShapeDtypeStruct(gradient.shape, jnp.float32),
        in_specs=[pl.BlockSpec(memory_space=pltpu.HBM)] * 3,
        out_specs=pl.BlockSpec(memory_space=pltpu.VMEM),
        scratch_shapes=[
            pltpu.VMEM((per_mem, mem_count, rows, cols), jnp.bfloat16),
            pltpu.VMEM((mem_count, per_mem, full_rows, full_cols), jnp.float32),
            pltpu.VMEM((2, mem_count, packed, cols), jnp.bfloat16),
            pltpu.VMEM((2, mem_count, rows, LANES), jnp.bfloat16),
            pltpu.VMEM((2, mem_count, packed, cols + 2 * LANES), jnp.bfloat16),
            pltpu.VMEM((2, mem_count, rows, LANES), jnp.bfloat16),
            pltpu.VMEM((5, rows + 2 * SUB, cols + 2 * LANES), jnp.float32),
            pltpu.VMEM((9, full_rows, full_cols), jnp.float32),
            pltpu.VMEM((2, full_rows, full_cols), jnp.float32),
            pltpu.VMEM((mem_count, rows + 2 * SUB, cols + 2 * LANES), jnp.float32),
            pltpu.VMEM((mem_count, cols // LANES, rows, LANES), jnp.float32),
            pltpu.VMEM((mem_count, cols // LANES, full_rows, LANES), jnp.float32),
            pltpu.VMEM((max(5, per_mem), full_cols // LANES, full_rows, LANES), jnp.float32),
            pltpu.SemaphoreType.DMA((mem_count,)),
            pltpu.SemaphoreType.DMA((mem_count,)),
            pltpu.SemaphoreType.DMA((mem_count,)),
            pltpu.SemaphoreType.DMA((mem_count,)),
            pltpu.SemaphoreType.DMA((3, len(DIRECTIONS))),
            pltpu.SemaphoreType.DMA((3, len(DIRECTIONS))),
            pltpu.SemaphoreType.DMA((3,)),
        ],
        compiler_params=pltpu.CompilerParams(
            collective_id=0, has_side_effects=True, vmem_limit_bytes=55192 * 1024
        ),
    )(perturbations, gradient, filter_coef)


def solution(mesh):
    sizes = tuple(mesh.shape[name] for name in ("mem", "lat", "lon"))
    return jax.shard_map(
        functools.partial(body, sizes),
        mesh=mesh,
        in_specs=(P("mem", "lat", "lon"), P("mem", None, "lat", "lon"), P(None, "lat", "lon")),
        out_specs=P("mem", "lat", "lon"),
        check_vma=False,
    )
```

```python
import functools

import jax
import jax.numpy as jnp
from jax import lax
from jax.experimental import pallas as pl
from jax.experimental.pallas import tpu as pltpu
from jax.sharding import PartitionSpec as P

HALO = 4
LANES = 128
SUB = 8
DIRECTIONS = ((-1, 0), (1, 0), (0, -1), (0, 1), (-1, -1), (-1, 1), (1, -1), (1, 1))


def shifted(values, offset, axis):
    unit = (SUB, LANES)[axis]
    size = values.shape[axis]
    if offset < 0:
        edge = pltpu.roll(lax.slice_in_dim(values, size - unit, size, axis=axis), 1, axis)
        return jnp.concatenate([edge, lax.slice_in_dim(values, 0, size - unit, axis=axis)], axis=axis)
    edge = pltpu.roll(lax.slice_in_dim(values, 0, unit, axis=axis), unit - 1, axis)
    return jnp.concatenate([lax.slice_in_dim(values, unit, size, axis=axis), edge], axis=axis)


def moved(values, matrix):
    high = values.astype(jnp.bfloat16).astype(jnp.float32)
    rest = values - high
    middle = rest.astype(jnp.bfloat16).astype(jnp.float32)
    parts = jnp.concatenate([high, middle, rest - middle], axis=0).astype(jnp.bfloat16)
    result = jnp.dot(parts, matrix, preferred_element_type=jnp.float32)
    size = values.shape[0]
    return result[:size] + result[size : 2 * size] + result[2 * size :]


def place_of(index, unit, size):
    return (index % unit) * (size // unit) + index // unit


def columns_of(values):
    return [values[:, low : low + LANES] for low in range(0, values.shape[1], LANES)]


def interleaved(ref, values):
    tiles = values.shape[0] // SUB
    for u, column in enumerate(columns_of(values)):
        ref[u] = column
    return jnp.concatenate(
        [
            jnp.concatenate(
                [ref[u, pl.ds(t, SUB, stride=tiles), :] for t in range(tiles)], axis=0
            )
            for u in range(ref.shape[0])
        ],
        axis=1,
    )


def circular(centre_rows, north_rows, south_rows, row_low):
    return jnp.concatenate([centre_rows, jnp.where(row_low, south_rows, north_rows)], axis=0)


def folded(padded, cols):
    low = lax.broadcasted_iota(jnp.int32, (padded.shape[0], LANES), 1) < LANES // 2
    side = jnp.where(low, padded[:, LANES + cols :], padded[:, :LANES])
    return jnp.concatenate([padded[:, LANES : LANES + cols], side], axis=1)


def kernel(
    sizes,
    pert,
    grad,
    coef,
    out,
    centre,
    field,
    send_rows,
    send_cols,
    recv_rows,
    recv_cols,
    ext,
    stencils,
    scaled,
    level_grads,
    grads,
    sums,
    natural,
    perm_cols,
    back_cols,
    z_send,
    z_recv,
    sum_send,
    sum_recv,
    halo_send,
    halo_recv,
    local_sem,
):
    mem_count, lat_count, lon_count, scale = sizes
    per_mem, _, rows, cols = pert.shape
    mem, lat, lon = (lax.axis_index(name) for name in ("mem", "lat", "lon"))
    mesh_id = pl.DeviceIdType.MESH

    def present(direction):
        up, right = direction
        checks = []
        if up:
            checks.append(lat > 0 if up < 0 else lat < lat_count - 1)
        if right:
            checks.append(lon > 0 if right < 0 else lon < lon_count - 1)
        return functools.reduce(jnp.logical_and, checks)

    def neighbour(direction):
        return (mem, lat + direction[0], lon + direction[1])

    def peer(offset):
        total, bit = 0, 1
        while bit < mem_count:
            total = total + bit * lax.rem(lax.div(mem, bit) + lax.div(offset, bit), 2)
            bit *= 2
        return total

    def group_at(step):
        return lax.rem(step + 1, mem_count)

    barrier = pltpu.get_barrier_semaphore()
    for offset in range(1, mem_count):
        pl.semaphore_signal(barrier, inc=1, device_id=(peer(jnp.int32(offset)), lat, lon), device_id_type=mesh_id)
    for direction in DIRECTIONS:

        @pl.when(present(direction))
        def _():
            pl.semaphore_signal(barrier, inc=1, device_id=neighbour(direction), device_id_type=mesh_id)

    inner_rows, inner_cols = pl.ds(SUB, rows), pl.ds(LANES, cols)

    own_pert = pltpu.make_async_copy(pert, centre, local_sem.at[2])
    own_grad = pltpu.make_async_copy(
        grad.at[0], grads.at[0, inner_rows, inner_cols], local_sem.at[0]
    )
    own_coef = pltpu.make_async_copy(
        coef, ext.at[:, inner_rows, inner_cols], local_sem.at[1]
    )
    own_pert.start()
    own_grad.start()
    own_coef.start()

    full_rows, full_cols = rows + 2 * HALO, cols + LANES

    def inside_of(row_index, col_index):
        row_index = jnp.where(row_index < rows + HALO, row_index, row_index - full_rows)
        col_index = jnp.where(col_index < cols + LANES // 2, col_index, col_index - full_cols)
        near = (col_index >= -HALO) & (col_index < cols + HALO)
        row_index = row_index + lat * rows
        col_index = col_index + lon * cols
        return (
            near
            & (row_index >= 0)
            & (row_index < rows * lat_count)
            & (col_index >= 0)
            & (col_index < cols * lon_count)
        )

    row_index, col_index = (
        lax.broadcasted_iota(jnp.int32, (full_rows, full_cols), axis) for axis in range(2)
    )
    inside = inside_of(row_index, col_index)
    scaled[1] = inside.astype(jnp.float32)
    inside_here = inside_of(
        place_of(row_index, SUB, full_rows), place_of(col_index, LANES, full_cols)
    )

    place = place_of(lax.broadcasted_iota(jnp.int32, (1, full_cols), 1), LANES, full_cols)
    source = lax.broadcasted_iota(jnp.int32, perm_cols.shape, 0)
    perm_cols[...] = jnp.where(source == place, 1.0, 0.0).astype(jnp.bfloat16)
    place = place_of(lax.broadcasted_iota(jnp.int32, (full_cols, 1), 0), LANES, full_cols)
    target = lax.broadcasted_iota(jnp.int32, back_cols.shape, 1)
    back_cols[...] = jnp.where(target == place, 1.0, 0.0).astype(jnp.bfloat16)
    low_row_full = lax.broadcasted_iota(jnp.int32, (SUB, full_cols), 0) < HALO

    blocks = [
        1 + jnp.where(here > 0, 1, 0) + jnp.where(here < count - 1, 1, 0)
        for here, count in ((lat, lat_count), (lon, lon_count))
    ]
    pl.semaphore_wait(barrier, mem_count - 2 + blocks[0] * blocks[1])

    def across(offset):
        return pltpu.make_async_remote_copy(
            src_ref=grad.at[0],
            dst_ref=grads.at[offset, inner_rows, inner_cols],
            send_sem=z_send.at[offset],
            recv_sem=z_recv.at[offset],
            device_id=(peer(offset), lat, lon),
            device_id_type=mesh_id,
        )

    def back(offset):
        return pltpu.make_async_remote_copy(
            src_ref=sums.at[0, offset],
            dst_ref=sums.at[1, offset],
            send_sem=sum_send.at[offset],
            recv_sem=sum_recv.at[offset],
            device_id=(peer(offset), lat, lon),
            device_id_type=mesh_id,
        )

    for offset in range(1, mem_count):
        across(jnp.int32(offset)).start()

    def span(step, low, size, edge):
        if step == 0:
            return pl.ds(0, size), pl.ds(low, size)
        if step < 0:
            return pl.ds(0, edge), pl.ds(low + size, edge)
        return pl.ds(size - edge, edge), pl.ds(low - edge, edge)

    def coef_copy(number, direction):
        source_rows, target_rows = span(direction[0], SUB, rows, SUB)
        source_cols, target_cols = span(direction[1], LANES, cols, LANES)
        return pltpu.make_async_remote_copy(
            src_ref=coef.at[:, source_rows, source_cols],
            dst_ref=ext.at[:, target_rows, target_cols],
            send_sem=halo_send.at[0, number],
            recv_sem=halo_recv.at[0, number],
            device_id=neighbour(direction),
            device_id_type=mesh_id,
        )

    def grad_copy(number, direction):
        source_rows, target_rows = span(direction[0], SUB, rows, SUB)
        source_cols, target_cols = span(direction[1], LANES, cols, LANES)
        source_rows = pl.ds(source_rows.start + SUB, source_rows.size)
        source_cols = pl.ds(source_cols.start + LANES, source_cols.size)
        return pltpu.make_async_remote_copy(
            src_ref=grads.at[:, source_rows, source_cols],
            dst_ref=grads.at[:, target_rows, target_cols],
            send_sem=halo_send.at[1, number],
            recv_sem=halo_recv.at[1, number],
            device_id=neighbour(direction),
            device_id_type=mesh_id,
        )

    def pert_copy(number, direction):
        up, right = direction
        if up == 0:
            side = 0 if right < 0 else 1
            source, target = send_cols.at[side], recv_cols.at[side]
        else:
            side = 0 if up < 0 else 1
            source_cols, target_cols = span(right, LANES, cols, LANES)
            source = send_rows.at[side, :, :, source_cols]
            target = recv_rows.at[side, :, :, target_cols]
        return pltpu.make_async_remote_copy(
            src_ref=source,
            dst_ref=target,
            send_sem=halo_send.at[2, number],
            recv_sem=halo_recv.at[2, number],
            device_id=neighbour(direction),
            device_id_type=mesh_id,
        )

    def for_targets(action):
        for number, direction in enumerate(DIRECTIONS):

            @pl.when(present(direction))
            def _():
                action(number, direction)

    def for_sources(action):
        for number, direction in enumerate(DIRECTIONS):

            @pl.when(present((-direction[0], -direction[1])))
            def _():
                action(number, direction)

    for_targets(lambda number, direction: coef_copy(number, direction).start())

    low_row = lax.broadcasted_iota(jnp.int32, (SUB, cols), 0) < HALO
    lane = lax.broadcasted_iota(jnp.int32, (rows, LANES), 1)
    tiles = send_rows.shape[2] // SUB

    def pack(group, carry):
        tops, bottoms = [], []
        west = east = None
        for k in range(per_mem):
            block = centre[k, peer(group)].astype(jnp.float32)
            top, bottom = block[:SUB], block[rows - SUB :]
            if k % 2:
                tops[-1] = jnp.where(low_row, tops[-1], pltpu.roll(top, HALO, 0))
                bottoms[-1] = jnp.where(low_row, pltpu.roll(bottom, HALO, 0), bottoms[-1])
            else:
                tops.append(top)
                bottoms.append(bottom)
            place = (lane >= HALO * k) & (lane < HALO * (k + 1))
            first = pltpu.roll(block[:, :LANES], HALO * k, 1) if k else block[:, :LANES]
            last = pltpu.roll(block[:, cols - LANES :], HALO * (k + 1) % LANES, 1)
            west = first if west is None else jnp.where(place, first, west)
            east = last if east is None else jnp.where(place, last, east)
        while len(tops) < tiles:
            tops.append(tops[-1])
            bottoms.append(bottoms[-1])
        send_rows[0, group] = jnp.concatenate(tops, axis=0).astype(jnp.bfloat16)
        send_rows[1, group] = jnp.concatenate(bottoms, axis=0).astype(jnp.bfloat16)
        send_cols[0, group] = west.astype(jnp.bfloat16)
        send_cols[1, group] = east.astype(jnp.bfloat16)
        return carry

    own_pert.wait()
    lax.fori_loop(0, mem_count, pack, 0)
    for_targets(lambda number, direction: pert_copy(number, direction).start())
    own_coef.wait()
    for_sources(lambda number, direction: coef_copy(number, direction).wait_recv())

    def extended(blocks):
        stack = []
        for block in blocks:
            wide = folded(block, cols)
            wide = circular(
                wide[SUB : SUB + rows], wide[:SUB], wide[SUB + rows :], low_row_full
            )
            stack.append(jnp.where(scaled[1] > 0.5, wide, 0.0))
        stack = moved(jnp.concatenate(stack, axis=0), perm_cols[...])
        return [
            interleaved(natural.at[index], stack[index * full_rows : (index + 1) * full_rows])
            for index in range(len(blocks))
        ]

    c0, cn, cs, cw, ce = extended([ext[index] for index in range(5)])
    for index, value in enumerate((c0, cn, cs, cw, ce)):
        stencils[index] = value
    for index, value in enumerate(
        (shifted(cs, -1, 0), shifted(cn, 1, 0), shifted(ce, -1, 1), shifted(cw, 1, 1))
    ):
        stencils[5 + index] = jnp.where(inside_here, value, 0.0)

    def one_pass(values, first):
        total = stencils[0] * values + stencils[first] * shifted(values, -1, 0)
        total = total + stencils[first + 1] * shifted(values, 1, 0)
        total = total + stencils[first + 2] * shifted(values, -1, 1)
        return total + stencils[first + 3] * shifted(values, 1, 1)

    own_grad.wait()
    for offset in range(1, mem_count):
        across(jnp.int32(offset)).wait_recv()
    for_targets(lambda number, direction: grad_copy(number, direction).start())
    for_sources(lambda number, direction: pert_copy(number, direction).wait_recv())

    def build(group, carry):
        south = folded(recv_rows[0, group].astype(jnp.float32), cols)
        north = folded(recv_rows[1, group].astype(jnp.float32), cols)
        from_east = recv_cols[0, group].astype(jnp.float32)
        from_west = recv_cols[1, group].astype(jnp.float32)
        blocks = []
        for k in range(per_mem):
            block = centre[k, peer(group)].astype(jnp.float32)
            tile = slice((k // 2) * SUB, (k // 2 + 1) * SUB)
            south_rows, north_rows = south[tile], north[tile]
            if k % 2:
                south_rows = pltpu.roll(south_rows, HALO, 0)
                north_rows = pltpu.roll(north_rows, HALO, 0)
            east = pltpu.roll(from_east, LANES - HALO * k, 1) if k else from_east
            west = pltpu.roll(from_west, (-HALO * (k + 1)) % LANES, 1)
            side = jnp.where(lane < LANES // 2, east, west)
            block = circular(
                jnp.concatenate([block, side], axis=1), north_rows, south_rows, low_row_full
            )
            blocks.append(jnp.where(scaled[1] > 0.5, block, 0.0))
        stack = jnp.concatenate(blocks, axis=0).astype(jnp.bfloat16)
        stack = jnp.dot(stack, perm_cols[...], preferred_element_type=jnp.float32)
        for k in range(per_mem):
            block = stack[k * full_rows : (k + 1) * full_rows]
            field[group, k] = interleaved(natural.at[k], block)
        return carry

    lax.fori_loop(0, mem_count, build, 0)
    for_sources(lambda number, direction: grad_copy(number, direction).wait_recv())

    for index, value in enumerate(extended([grads[index] for index in range(mem_count)])):
        level_grads[index] = value

    def step_work(step, carry):
        group = group_at(step)
        total = jnp.zeros((full_rows, full_cols), jnp.float32)
        for k in range(per_mem):
            values = field[group, k] * level_grads[group]
            values = one_pass(values, 5)
            values = one_pass(values, 5)
            values = one_pass(values, 1)
            values = one_pass(values, 1)
            total = total + values * field[group, k]
        tiles = full_rows // SUB
        for u, column in enumerate(columns_of(total)):
            for t in range(tiles):
                natural[0, u, pl.ds(t, SUB, stride=tiles), :] = column[t * SUB : (t + 1) * SUB]
        total = jnp.concatenate(
            [natural[0, u, :rows, :] for u in range(full_cols // LANES)], axis=1
        )
        sums[0, group] = moved(total, back_cols[...])

        @pl.when(step + 1 < mem_count)
        def _():
            back(group).start()

        return carry

    lax.fori_loop(0, mem_count, step_work, 0)
    total = sums[0, 0]
    for offset in range(1, mem_count):
        back(jnp.int32(offset)).wait_recv()
        total = total + sums[1, offset]
    out[0] = total * scale

    for offset in range(1, mem_count):
        across(jnp.int32(offset)).wait_send()
        back(jnp.int32(offset)).wait_send()

    def sent(number, direction):
        for copy in (coef_copy, grad_copy, pert_copy):
            copy(number, direction).wait_send()

    for_targets(sent)


def body(mesh_sizes, gradient, perturbations, filter_coef):
    mem_count, lat_count, lon_count = mesh_sizes
    levels, rows, cols = gradient.shape
    per_mem = perturbations.shape[0]
    members = per_mem * mem_count
    assert mem_count & (mem_count - 1) == 0 and HALO * per_mem <= LANES
    assert levels == 1 and rows % 16 == 0 and cols % LANES == 0
    full_rows, full_cols = rows + 2 * HALO, cols + LANES
    packed = (per_mem + 3) // 4 * 2 * SUB
    sizes = (mem_count, lat_count, lon_count, 1.0 / (members - 1))
    return pl.pallas_call(
        functools.partial(kernel, sizes),
        out_shape=jax.ShapeDtypeStruct(gradient.shape, jnp.float32),
        in_specs=[pl.BlockSpec(memory_space=pltpu.HBM)] * 3,
        out_specs=pl.BlockSpec(memory_space=pltpu.VMEM),
        scratch_shapes=[
            pltpu.VMEM((per_mem, mem_count, rows, cols), jnp.bfloat16),
            pltpu.VMEM((mem_count, per_mem, full_rows, full_cols), jnp.float32),
            pltpu.VMEM((2, mem_count, packed, cols), jnp.bfloat16),
            pltpu.VMEM((2, mem_count, rows, LANES), jnp.bfloat16),
            pltpu.VMEM((2, mem_count, packed, cols + 2 * LANES), jnp.bfloat16),
            pltpu.VMEM((2, mem_count, rows, LANES), jnp.bfloat16),
            pltpu.VMEM((5, rows + 2 * SUB, cols + 2 * LANES), jnp.float32),
            pltpu.VMEM((9, full_rows, full_cols), jnp.float32),
            pltpu.VMEM((2, full_rows, full_cols), jnp.float32),
            pltpu.VMEM((mem_count, full_rows, full_cols), jnp.float32),
            pltpu.VMEM((mem_count, rows + 2 * SUB, cols + 2 * LANES), jnp.float32),
            pltpu.VMEM((2, mem_count, rows, cols), jnp.float32),
            pltpu.VMEM((max(5, per_mem, mem_count), full_cols // LANES, full_rows, LANES), jnp.float32),
            pltpu.VMEM((full_cols, full_cols), jnp.bfloat16),
            pltpu.VMEM((full_cols, cols), jnp.bfloat16),
            pltpu.SemaphoreType.DMA((mem_count,)),
            pltpu.SemaphoreType.DMA((mem_count,)),
            pltpu.SemaphoreType.DMA((mem_count,)),
            pltpu.SemaphoreType.DMA((mem_count,)),
            pltpu.SemaphoreType.DMA((3, len(DIRECTIONS))),
            pltpu.SemaphoreType.DMA((3, len(DIRECTIONS))),
            pltpu.SemaphoreType.DMA((3,)),
        ],
        compiler_params=pltpu.CompilerParams(
            collective_id=0, has_side_effects=True, vmem_limit_bytes=55192 * 1024
        ),
    )(perturbations, gradient, filter_coef)


def solution(mesh):
    sizes = tuple(mesh.shape[name] for name in ("mem", "lat", "lon"))
    return jax.shard_map(
        functools.partial(body, sizes),
        mesh=mesh,
        in_specs=(P("mem", "lat", "lon"), P("mem", None, "lat", "lon"), P(None, "lat", "lon")),
        out_specs=P("mem", "lat", "lon"),
        check_vma=False,
    )
```

```python
import functools

import jax
import jax.numpy as jnp
from jax import lax
from jax.experimental import pallas as pl
from jax.experimental.pallas import tpu as pltpu
from jax.sharding import PartitionSpec as P

HALO = 4
LANES = 128
SUB = 8
DIRECTIONS = ((-1, 0), (1, 0), (0, -1), (0, 1), (-1, -1), (-1, 1), (1, -1), (1, 1))


def shifted(values, offset, axis):
    unit = (SUB, LANES)[axis]
    size = values.shape[axis]
    if offset < 0:
        edge = pltpu.roll(lax.slice_in_dim(values, size - unit, size, axis=axis), 1, axis)
        return jnp.concatenate([edge, lax.slice_in_dim(values, 0, size - unit, axis=axis)], axis=axis)
    edge = pltpu.roll(lax.slice_in_dim(values, 0, unit, axis=axis), unit - 1, axis)
    return jnp.concatenate([lax.slice_in_dim(values, unit, size, axis=axis), edge], axis=axis)


def moved(values, matrix):
    high = values.astype(jnp.bfloat16).astype(jnp.float32)
    rest = values - high
    middle = rest.astype(jnp.bfloat16).astype(jnp.float32)
    parts = jnp.concatenate([high, middle, rest - middle], axis=0).astype(jnp.bfloat16)
    result = jnp.dot(parts, matrix, preferred_element_type=jnp.float32)
    size = values.shape[0]
    return result[:size] + result[size : 2 * size] + result[2 * size :]


def place_of(index, unit, size):
    return (index % unit) * (size // unit) + index // unit


def columns_of(values):
    return [values[:, low : low + LANES] for low in range(0, values.shape[1], LANES)]


def interleaved(ref, values):
    tiles = values.shape[0] // SUB
    for u, column in enumerate(columns_of(values)):
        ref[u] = column
    return jnp.concatenate(
        [
            jnp.concatenate(
                [ref[u, pl.ds(t, SUB, stride=tiles), :] for t in range(tiles)], axis=0
            )
            for u in range(ref.shape[0])
        ],
        axis=1,
    )


def circular(centre_rows, north_rows, south_rows, row_low):
    return jnp.concatenate([centre_rows, jnp.where(row_low, south_rows, north_rows)], axis=0)


def folded(padded, cols):
    low = lax.broadcasted_iota(jnp.int32, (padded.shape[0], LANES), 1) < LANES // 2
    side = jnp.where(low, padded[:, LANES + cols :], padded[:, :LANES])
    return jnp.concatenate([padded[:, LANES : LANES + cols], side], axis=1)


def kernel(
    sizes,
    pert,
    grad,
    coef,
    out,
    centre,
    field,
    send_rows,
    send_cols,
    recv_rows,
    recv_cols,
    ext,
    stencils,
    scaled,
    level_grads,
    grads,
    sums,
    natural,
    perm_cols,
    back_cols,
    z_send,
    z_recv,
    sum_send,
    sum_recv,
    halo_send,
    halo_recv,
    local_sem,
):
    mem_count, lat_count, lon_count, scale = sizes
    per_mem, _, rows, cols = pert.shape
    mem, lat, lon = (lax.axis_index(name) for name in ("mem", "lat", "lon"))
    mesh_id = pl.DeviceIdType.MESH

    def present(direction):
        up, right = direction
        checks = []
        if up:
            checks.append(lat > 0 if up < 0 else lat < lat_count - 1)
        if right:
            checks.append(lon > 0 if right < 0 else lon < lon_count - 1)
        return functools.reduce(jnp.logical_and, checks)

    def neighbour(direction):
        return (mem, lat + direction[0], lon + direction[1])

    def peer(offset):
        total, bit = 0, 1
        while bit < mem_count:
            total = total + bit * lax.rem(lax.div(mem, bit) + lax.div(offset, bit), 2)
            bit *= 2
        return total

    def group_at(step):
        return lax.rem(step + 1, mem_count)

    barrier = pltpu.get_barrier_semaphore()
    for offset in range(1, mem_count):
        pl.semaphore_signal(barrier, inc=1, device_id=(peer(jnp.int32(offset)), lat, lon), device_id_type=mesh_id)
    for direction in DIRECTIONS:

        @pl.when(present(direction))
        def _():
            pl.semaphore_signal(barrier, inc=1, device_id=neighbour(direction), device_id_type=mesh_id)

    inner_rows, inner_cols = pl.ds(SUB, rows), pl.ds(LANES, cols)

    own_pert = pltpu.make_async_copy(pert, centre, local_sem.at[2])
    own_grad = pltpu.make_async_copy(
        grad.at[0], grads.at[0, inner_rows, inner_cols], local_sem.at[0]
    )
    own_coef = pltpu.make_async_copy(
        coef, ext.at[:, inner_rows, inner_cols], local_sem.at[1]
    )
    own_pert.start()
    own_grad.start()
    own_coef.start()

    blocks = [
        1 + jnp.where(here > 0, 1, 0) + jnp.where(here < count - 1, 1, 0)
        for here, count in ((lat, lat_count), (lon, lon_count))
    ]
    pl.semaphore_wait(barrier, mem_count - 2 + blocks[0] * blocks[1])

    def across(offset):
        return pltpu.make_async_remote_copy(
            src_ref=grad.at[0],
            dst_ref=grads.at[offset, inner_rows, inner_cols],
            send_sem=z_send.at[offset],
            recv_sem=z_recv.at[offset],
            device_id=(peer(offset), lat, lon),
            device_id_type=mesh_id,
        )

    def back(offset):
        return pltpu.make_async_remote_copy(
            src_ref=sums.at[0, offset],
            dst_ref=sums.at[1, offset],
            send_sem=sum_send.at[offset],
            recv_sem=sum_recv.at[offset],
            device_id=(peer(offset), lat, lon),
            device_id_type=mesh_id,
        )

    for offset in range(1, mem_count):
        across(jnp.int32(offset)).start()

    def span(step, low, size, edge):
        if step == 0:
            return pl.ds(0, size), pl.ds(low, size)
        if step < 0:
            return pl.ds(0, edge), pl.ds(low + size, edge)
        return pl.ds(size - edge, edge), pl.ds(low - edge, edge)

    def coef_copy(number, direction):
        source_rows, target_rows = span(direction[0], SUB, rows, SUB)
        source_cols, target_cols = span(direction[1], LANES, cols, LANES)
        return pltpu.make_async_remote_copy(
            src_ref=coef.at[:, source_rows, source_cols],
            dst_ref=ext.at[:, target_rows, target_cols],
            send_sem=halo_send.at[0, number],
            recv_sem=halo_recv.at[0, number],
            device_id=neighbour(direction),
            device_id_type=mesh_id,
        )

    def grad_copy(number, direction):
        source_rows, target_rows = span(direction[0], SUB, rows, SUB)
        source_cols, target_cols = span(direction[1], LANES, cols, LANES)
        source_rows = pl.ds(source_rows.start + SUB, source_rows.size)
        source_cols = pl.ds(source_cols.start + LANES, source_cols.size)
        return pltpu.make_async_remote_copy(
            src_ref=grads.at[:, source_rows, source_cols],
            dst_ref=grads.at[:, target_rows, target_cols],
            send_sem=halo_send.at[1, number],
            recv_sem=halo_recv.at[1, number],
            device_id=neighbour(direction),
            device_id_type=mesh_id,
        )

    def pert_copy(number, direction):
        up, right = direction
        if up == 0:
            side = 0 if right < 0 else 1
            source, target = send_cols.at[side], recv_cols.at[side]
        else:
            side = 0 if up < 0 else 1
            source_cols, target_cols = span(right, LANES, cols, LANES)
            source = send_rows.at[side, :, :, source_cols]
            target = recv_rows.at[side, :, :, target_cols]
        return pltpu.make_async_remote_copy(
            src_ref=source,
            dst_ref=target,
            send_sem=halo_send.at[2, number],
            recv_sem=halo_recv.at[2, number],
            device_id=neighbour(direction),
            device_id_type=mesh_id,
        )

    def for_targets(action):
        for number, direction in enumerate(DIRECTIONS):

            @pl.when(present(direction))
            def _():
                action(number, direction)

    def for_sources(action):
        for number, direction in enumerate(DIRECTIONS):

            @pl.when(present((-direction[0], -direction[1])))
            def _():
                action(number, direction)

    for_targets(lambda number, direction: coef_copy(number, direction).start())

    full_rows, full_cols = rows + 2 * HALO, cols + LANES

    def inside_of(row_index, col_index):
        row_index = jnp.where(row_index < rows + HALO, row_index, row_index - full_rows)
        col_index = jnp.where(col_index < cols + LANES // 2, col_index, col_index - full_cols)
        near = (col_index >= -HALO) & (col_index < cols + HALO)
        row_index = row_index + lat * rows
        col_index = col_index + lon * cols
        return (
            near
            & (row_index >= 0)
            & (row_index < rows * lat_count)
            & (col_index >= 0)
            & (col_index < cols * lon_count)
        )

    row_index, col_index = (
        lax.broadcasted_iota(jnp.int32, (full_rows, full_cols), axis) for axis in range(2)
    )
    inside = inside_of(row_index, col_index)
    scaled[1] = inside.astype(jnp.float32)
    inside_here = inside_of(
        place_of(row_index, SUB, full_rows), place_of(col_index, LANES, full_cols)
    )

    place = place_of(lax.broadcasted_iota(jnp.int32, (1, full_cols), 1), LANES, full_cols)
    source = lax.broadcasted_iota(jnp.int32, perm_cols.shape, 0)
    perm_cols[...] = jnp.where(source == place, 1.0, 0.0).astype(jnp.bfloat16)
    place = place_of(lax.broadcasted_iota(jnp.int32, (full_cols, 1), 0), LANES, full_cols)
    target = lax.broadcasted_iota(jnp.int32, back_cols.shape, 1)
    back_cols[...] = jnp.where(target == place, 1.0, 0.0).astype(jnp.bfloat16)
    low_row_full = lax.broadcasted_iota(jnp.int32, (SUB, full_cols), 0) < HALO

    low_row = lax.broadcasted_iota(jnp.int32, (SUB, cols), 0) < HALO
    lane = lax.broadcasted_iota(jnp.int32, (rows, LANES), 1)
    tiles = send_rows.shape[2] // SUB

    def pack(group, carry):
        tops, bottoms = [], []
        west = east = None
        for k in range(per_mem):
            block = centre[k, peer(group)].astype(jnp.float32)
            top, bottom = block[:SUB], block[rows - SUB :]
            if k % 2:
                tops[-1] = jnp.where(low_row, tops[-1], pltpu.roll(top, HALO, 0))
                bottoms[-1] = jnp.where(low_row, pltpu.roll(bottom, HALO, 0), bottoms[-1])
            else:
                tops.append(top)
                bottoms.append(bottom)
            place = (lane >= HALO * k) & (lane < HALO * (k + 1))
            first = pltpu.roll(block[:, :LANES], HALO * k, 1) if k else block[:, :LANES]
            last = pltpu.roll(block[:, cols - LANES :], HALO * (k + 1) % LANES, 1)
            west = first if west is None else jnp.where(place, first, west)
            east = last if east is None else jnp.where(place, last, east)
        while len(tops) < tiles:
            tops.append(tops[-1])
            bottoms.append(bottoms[-1])
        send_rows[0, group] = jnp.concatenate(tops, axis=0).astype(jnp.bfloat16)
        send_rows[1, group] = jnp.concatenate(bottoms, axis=0).astype(jnp.bfloat16)
        send_cols[0, group] = west.astype(jnp.bfloat16)
        send_cols[1, group] = east.astype(jnp.bfloat16)
        return carry

    own_pert.wait()
    lax.fori_loop(0, mem_count, pack, 0)
    for_targets(lambda number, direction: pert_copy(number, direction).start())
    own_coef.wait()
    for_sources(lambda number, direction: coef_copy(number, direction).wait_recv())

    def extended(blocks):
        stack = []
        for block in blocks:
            wide = folded(block, cols)
            wide = circular(
                wide[SUB : SUB + rows], wide[:SUB], wide[SUB + rows :], low_row_full
            )
            stack.append(jnp.where(scaled[1] > 0.5, wide, 0.0))
        stack = moved(jnp.concatenate(stack, axis=0), perm_cols[...])
        return [
            interleaved(natural.at[index], stack[index * full_rows : (index + 1) * full_rows])
            for index in range(len(blocks))
        ]

    c0, cn, cs, cw, ce = extended([ext[index] for index in range(5)])
    for index, value in enumerate((c0, cn, cs, cw, ce)):
        stencils[index] = value
    for index, value in enumerate(
        (shifted(cs, -1, 0), shifted(cn, 1, 0), shifted(ce, -1, 1), shifted(cw, 1, 1))
    ):
        stencils[5 + index] = jnp.where(inside_here, value, 0.0)

    def one_pass(values, first):
        total = stencils[0] * values + stencils[first] * shifted(values, -1, 0)
        total = total + stencils[first + 1] * shifted(values, 1, 0)
        total = total + stencils[first + 2] * shifted(values, -1, 1)
        return total + stencils[first + 3] * shifted(values, 1, 1)

    for_sources(lambda number, direction: pert_copy(number, direction).wait_recv())

    def build(group, carry):
        south = folded(recv_rows[0, group].astype(jnp.float32), cols)
        north = folded(recv_rows[1, group].astype(jnp.float32), cols)
        from_east = recv_cols[0, group].astype(jnp.float32)
        from_west = recv_cols[1, group].astype(jnp.float32)
        blocks = []
        for k in range(per_mem):
            block = centre[k, peer(group)].astype(jnp.float32)
            tile = slice((k // 2) * SUB, (k // 2 + 1) * SUB)
            south_rows, north_rows = south[tile], north[tile]
            if k % 2:
                south_rows = pltpu.roll(south_rows, HALO, 0)
                north_rows = pltpu.roll(north_rows, HALO, 0)
            east = pltpu.roll(from_east, LANES - HALO * k, 1) if k else from_east
            west = pltpu.roll(from_west, (-HALO * (k + 1)) % LANES, 1)
            side = jnp.where(lane < LANES // 2, east, west)
            block = circular(
                jnp.concatenate([block, side], axis=1), north_rows, south_rows, low_row_full
            )
            blocks.append(jnp.where(scaled[1] > 0.5, block, 0.0))
        stack = jnp.concatenate(blocks, axis=0).astype(jnp.bfloat16)
        stack = jnp.dot(stack, perm_cols[...], preferred_element_type=jnp.float32)
        for k in range(per_mem):
            block = stack[k * full_rows : (k + 1) * full_rows]
            field[group, k] = interleaved(natural.at[k], block)
        return carry

    early = mem_count // 2
    lax.fori_loop(0, early, build, 0)
    own_grad.wait()
    for offset in range(1, mem_count):
        across(jnp.int32(offset)).wait_recv()
    for_targets(lambda number, direction: grad_copy(number, direction).start())
    lax.fori_loop(early, mem_count, build, 0)
    for_sources(lambda number, direction: grad_copy(number, direction).wait_recv())

    for index, value in enumerate(extended([grads[index] for index in range(mem_count)])):
        level_grads[index] = value

    def step_work(step, carry):
        group = group_at(step)
        total = jnp.zeros((full_rows, full_cols), jnp.float32)
        for k in range(per_mem):
            values = field[group, k] * level_grads[group]
            values = one_pass(values, 5)
            values = one_pass(values, 5)
            values = one_pass(values, 1)
            values = one_pass(values, 1)
            total = total + values * field[group, k]
        tiles = full_rows // SUB
        for u, column in enumerate(columns_of(total)):
            for t in range(tiles):
                natural[0, u, pl.ds(t, SUB, stride=tiles), :] = column[t * SUB : (t + 1) * SUB]
        total = jnp.concatenate(
            [natural[0, u, :rows, :] for u in range(full_cols // LANES)], axis=1
        )
        sums[0, group] = moved(total, back_cols[...])

        @pl.when(step + 1 < mem_count)
        def _():
            back(group).start()

        return carry

    lax.fori_loop(0, mem_count, step_work, 0)
    total = sums[0, 0]
    for offset in range(1, mem_count):
        back(jnp.int32(offset)).wait_recv()
        total = total + sums[1, offset]
    out[0] = total * scale

    for offset in range(1, mem_count):
        across(jnp.int32(offset)).wait_send()
        back(jnp.int32(offset)).wait_send()

    def sent(number, direction):
        for copy in (coef_copy, grad_copy, pert_copy):
            copy(number, direction).wait_send()

    for_targets(sent)


def body(mesh_sizes, gradient, perturbations, filter_coef):
    mem_count, lat_count, lon_count = mesh_sizes
    levels, rows, cols = gradient.shape
    per_mem = perturbations.shape[0]
    members = per_mem * mem_count
    assert mem_count & (mem_count - 1) == 0 and HALO * per_mem <= LANES
    assert levels == 1 and rows % 16 == 0 and cols % LANES == 0
    full_rows, full_cols = rows + 2 * HALO, cols + LANES
    packed = (per_mem + 3) // 4 * 2 * SUB
    sizes = (mem_count, lat_count, lon_count, 1.0 / (members - 1))
    return pl.pallas_call(
        functools.partial(kernel, sizes),
        out_shape=jax.ShapeDtypeStruct(gradient.shape, jnp.float32),
        in_specs=[pl.BlockSpec(memory_space=pltpu.HBM)] * 3,
        out_specs=pl.BlockSpec(memory_space=pltpu.VMEM),
        scratch_shapes=[
            pltpu.VMEM((per_mem, mem_count, rows, cols), jnp.bfloat16),
            pltpu.VMEM((mem_count, per_mem, full_rows, full_cols), jnp.float32),
            pltpu.VMEM((2, mem_count, packed, cols), jnp.bfloat16),
            pltpu.VMEM((2, mem_count, rows, LANES), jnp.bfloat16),
            pltpu.VMEM((2, mem_count, packed, cols + 2 * LANES), jnp.bfloat16),
            pltpu.VMEM((2, mem_count, rows, LANES), jnp.bfloat16),
            pltpu.VMEM((5, rows + 2 * SUB, cols + 2 * LANES), jnp.float32),
            pltpu.VMEM((9, full_rows, full_cols), jnp.float32),
            pltpu.VMEM((2, full_rows, full_cols), jnp.float32),
            pltpu.VMEM((mem_count, full_rows, full_cols), jnp.float32),
            pltpu.VMEM((mem_count, rows + 2 * SUB, cols + 2 * LANES), jnp.float32),
            pltpu.VMEM((2, mem_count, rows, cols), jnp.float32),
            pltpu.VMEM((max(5, per_mem, mem_count), full_cols // LANES, full_rows, LANES), jnp.float32),
            pltpu.VMEM((full_cols, full_cols), jnp.bfloat16),
            pltpu.VMEM((full_cols, cols), jnp.bfloat16),
            pltpu.SemaphoreType.DMA((mem_count,)),
            pltpu.SemaphoreType.DMA((mem_count,)),
            pltpu.SemaphoreType.DMA((mem_count,)),
            pltpu.SemaphoreType.DMA((mem_count,)),
            pltpu.SemaphoreType.DMA((3, len(DIRECTIONS))),
            pltpu.SemaphoreType.DMA((3, len(DIRECTIONS))),
            pltpu.SemaphoreType.DMA((3,)),
        ],
        compiler_params=pltpu.CompilerParams(
            collective_id=0, has_side_effects=True, vmem_limit_bytes=55192 * 1024
        ),
    )(perturbations, gradient, filter_coef)


def solution(mesh):
    sizes = tuple(mesh.shape[name] for name in ("mem", "lat", "lon"))
    return jax.shard_map(
        functools.partial(body, sizes),
        mesh=mesh,
        in_specs=(P("mem", "lat", "lon"), P("mem", None, "lat", "lon"), P(None, "lat", "lon")),
        out_specs=P("mem", "lat", "lon"),
        check_vma=False,
    )
```

```python
import functools

import jax
import jax.numpy as jnp
from jax import lax
from jax.experimental import pallas as pl
from jax.experimental.pallas import tpu as pltpu
from jax.sharding import PartitionSpec as P

HALO = 4
LANES = 128
SUB = 8
DIRECTIONS = ((-1, 0), (1, 0), (0, -1), (0, 1), (-1, -1), (-1, 1), (1, -1), (1, 1))


def shifted(values, offset, axis):
    unit = (SUB, LANES)[axis]
    size = values.shape[axis]
    if offset < 0:
        edge = pltpu.roll(lax.slice_in_dim(values, size - unit, size, axis=axis), 1, axis)
        return jnp.concatenate([edge, lax.slice_in_dim(values, 0, size - unit, axis=axis)], axis=axis)
    edge = pltpu.roll(lax.slice_in_dim(values, 0, unit, axis=axis), unit - 1, axis)
    return jnp.concatenate([lax.slice_in_dim(values, unit, size, axis=axis), edge], axis=axis)


def moved(values, matrix):
    high = values.astype(jnp.bfloat16).astype(jnp.float32)
    rest = values - high
    middle = rest.astype(jnp.bfloat16).astype(jnp.float32)
    parts = jnp.concatenate([high, middle, rest - middle], axis=0).astype(jnp.bfloat16)
    result = jnp.dot(parts, matrix, preferred_element_type=jnp.float32)
    size = values.shape[0]
    return result[:size] + result[size : 2 * size] + result[2 * size :]


def place_of(index, unit, size):
    return (index % unit) * (size // unit) + index // unit


def columns_of(values):
    return [values[:, low : low + LANES] for low in range(0, values.shape[1], LANES)]


def interleaved(ref, values):
    tiles = values.shape[0] // SUB
    for u, column in enumerate(columns_of(values)):
        ref[u] = column
    return jnp.concatenate(
        [
            jnp.concatenate(
                [ref[u, pl.ds(t, SUB, stride=tiles), :] for t in range(tiles)], axis=0
            )
            for u in range(ref.shape[0])
        ],
        axis=1,
    )


def circular(centre_rows, north_rows, south_rows, row_low):
    return jnp.concatenate([centre_rows, jnp.where(row_low, south_rows, north_rows)], axis=0)


def folded(padded, cols):
    low = lax.broadcasted_iota(jnp.int32, (padded.shape[0], LANES), 1) < LANES // 2
    side = jnp.where(low, padded[:, LANES + cols :], padded[:, :LANES])
    return jnp.concatenate([padded[:, LANES : LANES + cols], side], axis=1)


def kernel(
    sizes,
    pert,
    grad,
    coef,
    out,
    centre,
    field,
    send_rows,
    send_cols,
    recv_rows,
    recv_cols,
    ext,
    stencils,
    scaled,
    level_grads,
    grads,
    sums,
    natural,
    perm_cols,
    back_cols,
    z_send,
    z_recv,
    sum_send,
    sum_recv,
    halo_send,
    halo_recv,
    local_sem,
):
    mem_count, lat_count, lon_count, scale = sizes
    per_mem, _, rows, cols = pert.shape
    mem, lat, lon = (lax.axis_index(name) for name in ("mem", "lat", "lon"))
    mesh_id = pl.DeviceIdType.MESH

    def present(direction):
        up, right = direction
        checks = []
        if up:
            checks.append(lat > 0 if up < 0 else lat < lat_count - 1)
        if right:
            checks.append(lon > 0 if right < 0 else lon < lon_count - 1)
        return functools.reduce(jnp.logical_and, checks)

    def neighbour(direction):
        return (mem, lat + direction[0], lon + direction[1])

    def peer(offset):
        total, bit = 0, 1
        while bit < mem_count:
            total = total + bit * lax.rem(lax.div(mem, bit) + lax.div(offset, bit), 2)
            bit *= 2
        return total

    def group_at(step):
        return lax.rem(step + 1, mem_count)

    barrier = pltpu.get_barrier_semaphore()
    for offset in range(1, mem_count):
        pl.semaphore_signal(barrier, inc=1, device_id=(peer(jnp.int32(offset)), lat, lon), device_id_type=mesh_id)
    for direction in DIRECTIONS:

        @pl.when(present(direction))
        def _():
            pl.semaphore_signal(barrier, inc=1, device_id=neighbour(direction), device_id_type=mesh_id)

    inner_rows, inner_cols = pl.ds(SUB, rows), pl.ds(LANES, cols)

    own_pert = pltpu.make_async_copy(pert, centre, local_sem.at[2])
    own_grad = pltpu.make_async_copy(
        grad.at[0], grads.at[0, inner_rows, inner_cols], local_sem.at[0]
    )
    own_coef = pltpu.make_async_copy(
        coef, ext.at[:, inner_rows, inner_cols], local_sem.at[1]
    )
    own_pert.start()
    own_grad.start()
    own_coef.start()

    full_rows, full_cols = rows + 2 * HALO, cols + LANES

    def inside_of(row_index, col_index):
        row_index = jnp.where(row_index < rows + HALO, row_index, row_index - full_rows)
        col_index = jnp.where(col_index < cols + LANES // 2, col_index, col_index - full_cols)
        near = (col_index >= -HALO) & (col_index < cols + HALO)
        row_index = row_index + lat * rows
        col_index = col_index + lon * cols
        return (
            near
            & (row_index >= 0)
            & (row_index < rows * lat_count)
            & (col_index >= 0)
            & (col_index < cols * lon_count)
        )

    row_index, col_index = (
        lax.broadcasted_iota(jnp.int32, (full_rows, full_cols), axis) for axis in range(2)
    )
    inside = inside_of(row_index, col_index)
    scaled[1] = inside.astype(jnp.float32)
    inside_here = inside_of(
        place_of(row_index, SUB, full_rows), place_of(col_index, LANES, full_cols)
    )

    place = place_of(lax.broadcasted_iota(jnp.int32, (1, full_cols), 1), LANES, full_cols)
    source = lax.broadcasted_iota(jnp.int32, perm_cols.shape, 0)
    perm_cols[...] = jnp.where(source == place, 1.0, 0.0).astype(jnp.bfloat16)
    place = place_of(lax.broadcasted_iota(jnp.int32, (full_cols, 1), 0), LANES, full_cols)
    target = lax.broadcasted_iota(jnp.int32, back_cols.shape, 1)
    back_cols[...] = jnp.where(target == place, 1.0, 0.0).astype(jnp.bfloat16)
    low_row_full = lax.broadcasted_iota(jnp.int32, (SUB, full_cols), 0) < HALO

    blocks = [
        1 + jnp.where(here > 0, 1, 0) + jnp.where(here < count - 1, 1, 0)
        for here, count in ((lat, lat_count), (lon, lon_count))
    ]
    pl.semaphore_wait(barrier, mem_count - 2 + blocks[0] * blocks[1])

    def across(offset):
        return pltpu.make_async_remote_copy(
            src_ref=grad.at[0],
            dst_ref=grads.at[offset, inner_rows, inner_cols],
            send_sem=z_send.at[offset],
            recv_sem=z_recv.at[offset],
            device_id=(peer(offset), lat, lon),
            device_id_type=mesh_id,
        )

    def back(offset):
        return pltpu.make_async_remote_copy(
            src_ref=sums.at[0, offset],
            dst_ref=sums.at[1, offset],
            send_sem=sum_send.at[offset],
            recv_sem=sum_recv.at[offset],
            device_id=(peer(offset), lat, lon),
            device_id_type=mesh_id,
        )

    for offset in range(1, mem_count):
        across(jnp.int32(offset)).start()

    def span(step, low, size, edge):
        if step == 0:
            return pl.ds(0, size), pl.ds(low, size)
        if step < 0:
            return pl.ds(0, edge), pl.ds(low + size, edge)
        return pl.ds(size - edge, edge), pl.ds(low - edge, edge)

    def coef_copy(number, direction):
        source_rows, target_rows = span(direction[0], SUB, rows, SUB)
        source_cols, target_cols = span(direction[1], LANES, cols, LANES)
        return pltpu.make_async_remote_copy(
            src_ref=coef.at[:, source_rows, source_cols],
            dst_ref=ext.at[:, target_rows, target_cols],
            send_sem=halo_send.at[0, number],
            recv_sem=halo_recv.at[0, number],
            device_id=neighbour(direction),
            device_id_type=mesh_id,
        )

    def grad_copy(number, direction):
        source_rows, target_rows = span(direction[0], SUB, rows, SUB)
        source_cols, target_cols = span(direction[1], LANES, cols, LANES)
        source_rows = pl.ds(source_rows.start + SUB, source_rows.size)
        source_cols = pl.ds(source_cols.start + LANES, source_cols.size)
        return pltpu.make_async_remote_copy(
            src_ref=grads.at[:, source_rows, source_cols],
            dst_ref=grads.at[:, target_rows, target_cols],
            send_sem=halo_send.at[1, number],
            recv_sem=halo_recv.at[1, number],
            device_id=neighbour(direction),
            device_id_type=mesh_id,
        )

    def pert_copy(number, direction):
        up, right = direction
        if up == 0:
            side = 0 if right < 0 else 1
            source, target = send_cols.at[side], recv_cols.at[side]
        else:
            side = 0 if up < 0 else 1
            source_cols, target_cols = span(right, LANES, cols, LANES)
            source = send_rows.at[side, :, :, source_cols]
            target = recv_rows.at[side, :, :, target_cols]
        return pltpu.make_async_remote_copy(
            src_ref=source,
            dst_ref=target,
            send_sem=halo_send.at[2, number],
            recv_sem=halo_recv.at[2, number],
            device_id=neighbour(direction),
            device_id_type=mesh_id,
        )

    def for_targets(action):
        for number, direction in enumerate(DIRECTIONS):

            @pl.when(present(direction))
            def _():
                action(number, direction)

    def for_sources(action):
        for number, direction in enumerate(DIRECTIONS):

            @pl.when(present((-direction[0], -direction[1])))
            def _():
                action(number, direction)

    for_targets(lambda number, direction: coef_copy(number, direction).start())

    low_row = lax.broadcasted_iota(jnp.int32, (SUB, cols), 0) < HALO
    lane = lax.broadcasted_iota(jnp.int32, (rows, LANES), 1)
    tiles = send_rows.shape[2] // SUB

    def pack(group, carry):
        tops, bottoms = [], []
        west = east = None
        for k in range(per_mem):
            block = centre[k, peer(group)].astype(jnp.float32)
            top, bottom = block[:SUB], block[rows - SUB :]
            if k % 2:
                tops[-1] = jnp.where(low_row, tops[-1], pltpu.roll(top, HALO, 0))
                bottoms[-1] = jnp.where(low_row, pltpu.roll(bottom, HALO, 0), bottoms[-1])
            else:
                tops.append(top)
                bottoms.append(bottom)
            place = (lane >= HALO * k) & (lane < HALO * (k + 1))
            first = pltpu.roll(block[:, :LANES], HALO * k, 1) if k else block[:, :LANES]
            last = pltpu.roll(block[:, cols - LANES :], HALO * (k + 1) % LANES, 1)
            west = first if west is None else jnp.where(place, first, west)
            east = last if east is None else jnp.where(place, last, east)
        while len(tops) < tiles:
            tops.append(tops[-1])
            bottoms.append(bottoms[-1])
        send_rows[0, group] = jnp.concatenate(tops, axis=0).astype(jnp.bfloat16)
        send_rows[1, group] = jnp.concatenate(bottoms, axis=0).astype(jnp.bfloat16)
        send_cols[0, group] = west.astype(jnp.bfloat16)
        send_cols[1, group] = east.astype(jnp.bfloat16)
        return carry

    own_pert.wait()
    lax.fori_loop(0, mem_count, pack, 0)
    for_targets(lambda number, direction: pert_copy(number, direction).start())
    own_grad.wait()
    for offset in range(1, mem_count):
        across(jnp.int32(offset)).wait_recv()
    for_targets(lambda number, direction: grad_copy(number, direction).start())
    own_coef.wait()
    for_sources(lambda number, direction: coef_copy(number, direction).wait_recv())

    def extended(blocks):
        stack = []
        for block in blocks:
            wide = folded(block, cols)
            wide = circular(
                wide[SUB : SUB + rows], wide[:SUB], wide[SUB + rows :], low_row_full
            )
            stack.append(jnp.where(scaled[1] > 0.5, wide, 0.0))
        stack = moved(jnp.concatenate(stack, axis=0), perm_cols[...])
        return [
            interleaved(natural.at[index], stack[index * full_rows : (index + 1) * full_rows])
            for index in range(len(blocks))
        ]

    c0, cn, cs, cw, ce = extended([ext[index] for index in range(5)])
    for index, value in enumerate((c0, cn, cs, cw, ce)):
        stencils[index] = value
    for index, value in enumerate(
        (shifted(cs, -1, 0), shifted(cn, 1, 0), shifted(ce, -1, 1), shifted(cw, 1, 1))
    ):
        stencils[5 + index] = jnp.where(inside_here, value, 0.0)

    def one_pass(values, first):
        total = stencils[0] * values + stencils[first] * shifted(values, -1, 0)
        total = total + stencils[first + 1] * shifted(values, 1, 0)
        total = total + stencils[first + 2] * shifted(values, -1, 1)
        return total + stencils[first + 3] * shifted(values, 1, 1)

    for_sources(lambda number, direction: pert_copy(number, direction).wait_recv())

    def build(group, carry):
        south = folded(recv_rows[0, group].astype(jnp.float32), cols)
        north = folded(recv_rows[1, group].astype(jnp.float32), cols)
        from_east = recv_cols[0, group].astype(jnp.float32)
        from_west = recv_cols[1, group].astype(jnp.float32)
        blocks = []
        for k in range(per_mem):
            block = centre[k, peer(group)].astype(jnp.float32)
            tile = slice((k // 2) * SUB, (k // 2 + 1) * SUB)
            south_rows, north_rows = south[tile], north[tile]
            if k % 2:
                south_rows = pltpu.roll(south_rows, HALO, 0)
                north_rows = pltpu.roll(north_rows, HALO, 0)
            east = pltpu.roll(from_east, LANES - HALO * k, 1) if k else from_east
            west = pltpu.roll(from_west, (-HALO * (k + 1)) % LANES, 1)
            side = jnp.where(lane < LANES // 2, east, west)
            block = circular(
                jnp.concatenate([block, side], axis=1), north_rows, south_rows, low_row_full
            )
            blocks.append(jnp.where(scaled[1] > 0.5, block, 0.0))
        stack = jnp.concatenate(blocks, axis=0).astype(jnp.bfloat16)
        stack = jnp.dot(stack, perm_cols[...], preferred_element_type=jnp.float32)
        for k in range(per_mem):
            block = stack[k * full_rows : (k + 1) * full_rows]
            field[group, k] = interleaved(natural.at[k], block)
        return carry

    lax.fori_loop(0, mem_count, build, 0)
    for_sources(lambda number, direction: grad_copy(number, direction).wait_recv())

    for index, value in enumerate(extended([grads[index] for index in range(mem_count)])):
        level_grads[index] = value

    def step_work(step, carry):
        group = group_at(step)
        total = jnp.zeros((full_rows, full_cols), jnp.float32)
        for k in range(per_mem):
            values = field[group, k] * level_grads[group]
            values = one_pass(values, 5)
            values = one_pass(values, 5)
            values = one_pass(values, 1)
            values = one_pass(values, 1)
            total = total + values * field[group, k]
        tiles = full_rows // SUB
        for u, column in enumerate(columns_of(total)):
            for t in range(tiles):
                natural[0, u, pl.ds(t, SUB, stride=tiles), :] = column[t * SUB : (t + 1) * SUB]
        total = jnp.concatenate(
            [natural[0, u, :rows, :] for u in range(full_cols // LANES)], axis=1
        )
        sums[0, group] = moved(total, back_cols[...])

        @pl.when(step + 1 < mem_count)
        def _():
            back(group).start()

        return carry

    lax.fori_loop(0, mem_count, step_work, 0)
    total = sums[0, 0]
    for offset in range(1, mem_count):
        back(jnp.int32(offset)).wait_recv()
        total = total + sums[1, offset]
    out[0] = total * scale

    for offset in range(1, mem_count):
        across(jnp.int32(offset)).wait_send()
        back(jnp.int32(offset)).wait_send()

    def sent(number, direction):
        for copy in (coef_copy, grad_copy, pert_copy):
            copy(number, direction).wait_send()

    for_targets(sent)


def body(mesh_sizes, gradient, perturbations, filter_coef):
    mem_count, lat_count, lon_count = mesh_sizes
    levels, rows, cols = gradient.shape
    per_mem = perturbations.shape[0]
    members = per_mem * mem_count
    assert mem_count & (mem_count - 1) == 0 and HALO * per_mem <= LANES
    assert levels == 1 and rows % 16 == 0 and cols % LANES == 0
    full_rows, full_cols = rows + 2 * HALO, cols + LANES
    packed = (per_mem + 3) // 4 * 2 * SUB
    sizes = (mem_count, lat_count, lon_count, 1.0 / (members - 1))
    return pl.pallas_call(
        functools.partial(kernel, sizes),
        out_shape=jax.ShapeDtypeStruct(gradient.shape, jnp.float32),
        in_specs=[pl.BlockSpec(memory_space=pltpu.HBM)] * 3,
        out_specs=pl.BlockSpec(memory_space=pltpu.VMEM),
        scratch_shapes=[
            pltpu.VMEM((per_mem, mem_count, rows, cols), jnp.bfloat16),
            pltpu.VMEM((mem_count, per_mem, full_rows, full_cols), jnp.float32),
            pltpu.VMEM((2, mem_count, packed, cols), jnp.bfloat16),
            pltpu.VMEM((2, mem_count, rows, LANES), jnp.bfloat16),
            pltpu.VMEM((2, mem_count, packed, cols + 2 * LANES), jnp.bfloat16),
            pltpu.VMEM((2, mem_count, rows, LANES), jnp.bfloat16),
            pltpu.VMEM((5, rows + 2 * SUB, cols + 2 * LANES), jnp.float32),
            pltpu.VMEM((9, full_rows, full_cols), jnp.float32),
            pltpu.VMEM((2, full_rows, full_cols), jnp.float32),
            pltpu.VMEM((mem_count, full_rows, full_cols), jnp.float32),
            pltpu.VMEM((mem_count, rows + 2 * SUB, cols + 2 * LANES), jnp.float32),
            pltpu.VMEM((2, mem_count, rows, cols), jnp.float32),
            pltpu.VMEM((max(5, per_mem, mem_count), full_cols // LANES, full_rows, LANES), jnp.float32),
            pltpu.VMEM((full_cols, full_cols), jnp.bfloat16),
            pltpu.VMEM((full_cols, cols), jnp.bfloat16),
            pltpu.SemaphoreType.DMA((mem_count,)),
            pltpu.SemaphoreType.DMA((mem_count,)),
            pltpu.SemaphoreType.DMA((mem_count,)),
            pltpu.SemaphoreType.DMA((mem_count,)),
            pltpu.SemaphoreType.DMA((3, len(DIRECTIONS))),
            pltpu.SemaphoreType.DMA((3, len(DIRECTIONS))),
            pltpu.SemaphoreType.DMA((3,)),
        ],
        compiler_params=pltpu.CompilerParams(
            collective_id=0, has_side_effects=True, vmem_limit_bytes=55192 * 1024
        ),
    )(perturbations, gradient, filter_coef)


def solution(mesh):
    sizes = tuple(mesh.shape[name] for name in ("mem", "lat", "lon"))
    return jax.shard_map(
        functools.partial(body, sizes),
        mesh=mesh,
        in_specs=(P("mem", "lat", "lon"), P("mem", None, "lat", "lon"), P(None, "lat", "lon")),
        out_specs=P("mem", "lat", "lon"),
        check_vma=False,
    )
```
